128 devices in a mesh: row: 8 (over x, core), col: 16 (over z, y).
Axes of the slice: x: 4, y: 4, z: 4, core: 2. Of those that a mesh axis runs over, the one named last changes fastest.
Arguments:
- values: bfloat16 [1024, 60416], P('col', 'row'), as said below
- pattern: int32 [944, 16], P(None, 'col'), may hold values from 0 to 943, as said below
Outputs:
- squared: bfloat16 [1024, 60416], P('col', 'row')
- updated: bfloat16 [1024, 60416], P('col', 'row')
The draws below stay inside these ranges and needn't reach their ends.
Inputs may be any that keep to these rules, and one draw needn't show every extreme that they name: pattern[r, g] lies in the group g * 59 to (g + 1) * 59 - 1; pattern[r, r // 59] = r; the pattern is symmetric: pattern[pattern[r, g], r // 59] = r. values define a symmetric matrix: the block stored for block row r in group g is exactly the transpose of the block stored for block row pattern[r, g] in group r // 59.
All inputs are finite; a program needn't handle non-finite values.
Results may differ from the reference program's by a relative error of at most 0.0047.
Values may be sent and summed in bfloat16 or wider, within the bound.
No kernel may reach another device: no remote copies, remote signals or barrier semaphores. Data moves between devices by JAX's collectives and lax.ppermute only.
A program may use at most 320 MiB of HBM per device.

```python
import math
import jax
import jax.numpy as jnp
from jax import lax

B = 64
NB = 944
GROUPS = 16


def one_order(subkey):
    return jax.random.permutation(subkey, NB // GROUPS)


def block_pattern(key):
    span_width = NB // GROUPS
    key_perm, key_shift, key_twist = jax.random.split(key, 3)
    orders = jax.vmap(one_order)(jax.random.split(key_perm, GROUPS)).astype(jnp.int32)
    labels = jnp.argsort(orders, axis=1).astype(jnp.int32)
    offsets = jax.random.randint(key_shift, (GROUPS,), 0, span_width, dtype=jnp.int32)
    twist = jax.random.randint(key_twist, (GROUPS, GROUPS), -1, 2, dtype=jnp.int32)
    upper = jnp.triu(twist, 1)
    twist = upper - upper.T
    shifts = offsets[None, :] - offsets[:, None] + twist
    row_ids = jnp.arange(NB, dtype=jnp.int32)
    home_group = row_ids // span_width
    position = row_ids % span_width
    row_label = labels[home_group, position]
    shifted = jnp.mod(row_label[:, None] + shifts[home_group, :], span_width).astype(jnp.int32)
    group_ids = jnp.arange(GROUPS, dtype=jnp.int32)
    return (group_ids[None, :] * span_width + orders[group_ids[None, :], shifted]).astype(jnp.int32)


def draw_pattern(key, part):
    return block_pattern(key)


def draw_values(key, part):
    pattern_links = block_pattern(key)
    key = jax.random.fold_in(key, 7)
    key_noise = jax.random.fold_in(key, 0)
    span_width = NB // GROUPS
    noise_blocks = jax.random.normal(key_noise, (GROUPS, NB, B, B), jnp.float32)
    row_ids = jnp.arange(NB, dtype=jnp.int32)
    home_group = row_ids // span_width
    partner = noise_blocks[home_group[None, :], pattern_links.T]
    symmetric = 0.5 * (noise_blocks + jnp.swapaxes(partner, 2, 3))
    return symmetric.transpose(0, 2, 1, 3).reshape(GROUPS * B, NB * B).astype(jnp.bfloat16)


def setup_inputs(seed: int = 0) -> dict:
    seeds = jax.random.split(jax.random.key(seed), 3)
    return {
        "values": draw_values(jax.random.fold_in(seeds[2], 71), 0),
        "pattern": draw_pattern(jax.random.fold_in(seeds[2], 71), 0),
    }


def stored_product(left, right, pattern):
    left_blocks = left.reshape(GROUPS, B, NB, B)
    right_blocks = right.reshape(GROUPS, B, NB, B).astype(jnp.float32)

    def one_group(group_index):
        column = lax.dynamic_index_in_dim(pattern, group_index, 1, keepdims=False)
        strips = lax.dynamic_index_in_dim(left_blocks, group_index, 0, keepdims=False)
        picked = strips[:, pattern, :].astype(jnp.float32)
        kept_mask = column[pattern] == column[:, None]
        picked = jnp.where(kept_mask[None, :, :, None], picked, jnp.zeros((), picked.dtype))
        return jnp.einsum('qcgt,gtcp->qcp', picked, right_blocks, precision=lax.Precision.HIGHEST)
    result = lax.map(one_group, jnp.arange(GROUPS, dtype=jnp.int32))
    return result.reshape(GROUPS * B, NB * B)

def reference(values, pattern):
    norm_scale = math.sqrt(GROUPS * B)
    squared = (stored_product(values, values, pattern) / norm_scale).astype(jnp.bfloat16)
    third_sum = stored_product(squared, values, pattern)
    updated = (1.5 * values.astype(jnp.float32) - 0.5 * third_sum / norm_scale).astype(jnp.bfloat16)
    return (squared, updated)
```

```python
import math

import jax
import jax.numpy as jnp
from jax import lax
from jax.experimental import pallas as pl
from jax.experimental.pallas import tpu as pltpu
from jax.sharding import PartitionSpec as P

STEPS = 4


def split_pairs(flat_ref, pair_ref, block):
    spans = pair_ref.shape[0]
    for m in range(spans):
        pair_ref[m, :, :block] = flat_ref[:, m * block : (m + 1) * block]
        pair_ref[m, :, block:] = flat_ref[:, (spans + m) * block : (spans + m + 1) * block]


def join_pairs(pair_ref, flat_ref, block):
    spans = pair_ref.shape[0]
    for m in range(spans):
        flat_ref[:, m * block : (m + 1) * block] = pair_ref[m, :, :block]
        flat_ref[:, (spans + m) * block : (spans + m + 1) * block] = pair_ref[m, :, block:]


def paired(array, spans):
    block = array.shape[0]

    def body(flat_ref, pair_ref):
        split_pairs(flat_ref, pair_ref, block)

    return pl.pallas_call(
        body,
        out_shape=jax.ShapeDtypeStruct((spans, block, 2 * block), array.dtype),
        compiler_params=pltpu.CompilerParams(vmem_limit_bytes=16 * 1024 * 1024),
    )(array)


def product_kernel(left_at, right_at, kept, left_ref, right_ref, *rest, block, scale, update):
    if update:
        own_ref, flat_ref, out_ref, total = rest
    else:
        flat_ref, out_ref, total = rest
    step = pl.program_id(0)
    spans = total.shape[0]
    pairs = left_ref.shape[0]
    groups = right_ref.shape[0]
    low = lax.broadcasted_iota(jnp.int32, (block, 2 * block), 1) < block

    def one(s, carry):
        left_parts = []
        for j in range(pairs):
            base = s * (STEPS * groups) + step * groups + 2 * j
            left_parts.append(jnp.where(low, left_ref[j, left_at[base]], left_ref[j, left_at[base + 1]]))
        left = jnp.concatenate(left_parts, axis=1)
        first, second = right_at[2 * s], right_at[2 * s + 1]
        right_parts = []
        for h in range(groups):
            flag = (s * (STEPS * groups) + step * groups + h) * 2
            picked = jnp.where(low, right_ref[h, first], right_ref[h, second])
            keep = jnp.where(low, kept[flag], kept[flag + 1]) != 0
            right_parts.append(jnp.where(keep, picked, jnp.zeros_like(picked)))
        right = jnp.concatenate(right_parts, axis=0)
        partial = jnp.dot(left, right, preferred_element_type=jnp.float32)

        @pl.when(step == 0)
        def _():
            total[s] = partial

        @pl.when(jnp.logical_and(step > 0, step < STEPS - 1))
        def _():
            total[s] += partial

        @pl.when(step == STEPS - 1)
        def _():
            summed = total[s] + partial
            if update:
                own = jnp.where(low, own_ref[first], own_ref[second]).astype(jnp.float32)
                result = (1.5 * own - (0.5 * scale) * summed).astype(out_ref.dtype)
            else:
                result = (summed * scale).astype(out_ref.dtype)
            out_ref[first, :, :block] = result[:, :block]
            out_ref[second, :, block:] = result[:, block:]

        return carry

    lax.fori_loop(0, spans, one, 0)

    @pl.when(step == STEPS - 1)
    def _():
        join_pairs(out_ref, flat_ref, block)


def product(left_at, right_at, kept, left, right, own, scale):
    pairs, spans, block, lanes = left.shape
    groups = right.shape[0]
    whole = pl.BlockSpec((spans, block, lanes), lambda i, *_: (0, 0, 0))
    flat = pl.BlockSpec((block, spans * lanes), lambda i, *_: (0, 0))
    in_specs = [
        pl.BlockSpec((pairs // STEPS, spans, block, lanes), lambda i, *_: (i, 0, 0, 0)),
        pl.BlockSpec((groups // STEPS, spans, block, lanes), lambda i, *_: (i, 0, 0, 0)),
    ]
    out_specs = [flat]
    out_shape = [jax.ShapeDtypeStruct((block, spans * lanes), jnp.bfloat16)]
    scratch_shapes = [pltpu.VMEM((spans, block, lanes), jnp.float32)]
    operands = [left, right]
    if own is not None:
        in_specs.append(whole)
        operands.append(own)
        scratch_shapes.insert(0, pltpu.VMEM((spans, block, lanes), jnp.bfloat16))
    else:
        out_specs.append(whole)
        out_shape.append(jax.ShapeDtypeStruct((spans, block, lanes), jnp.bfloat16))

    def body(*refs):
        product_kernel(*refs, block=block, scale=scale, update=own is not None)

    return pl.pallas_call(
        body,
        grid_spec=pltpu.PrefetchScalarGridSpec(
            num_scalar_prefetch=3,
            grid=(STEPS,),
            in_specs=in_specs,
            out_specs=out_specs,
            scratch_shapes=scratch_shapes,
        ),
        out_shape=out_shape,
        compiler_params=pltpu.CompilerParams(
            dimension_semantics=("arbitrary",), vmem_limit_bytes=48 * 1024 * 1024
        ),
        cost_estimate=pl.CostEstimate(
            flops=2 * spans * block * lanes * groups * block,
            bytes_accessed=2 * (left.size + right.size),
            transcendentals=0,
        ),
    )(left_at, right_at, kept, *operands)


def per_device(values, pattern):
    block = values.shape[0]
    rows_here = values.shape[1] // block
    groups = lax.axis_size("col")
    spans = pattern.shape[0] // groups
    mine = lax.axis_index("row")
    group = lax.axis_index("col")
    column = pattern[:, 0]

    own = paired(values, spans)
    own_links = lax.dynamic_slice_in_dim(column, mine * rows_here, rows_here, 0)
    links = lax.all_gather(own_links, "col", axis=0, tiled=False)
    left = lax.all_gather(own, "row", axis=0, tiled=False)
    right = lax.all_gather(own, "col", axis=0, tiled=False)

    order = jnp.arange(rows_here, dtype=jnp.int32) % spans
    targets = (own_links - group * spans).reshape(2, spans)
    member = jnp.arange(spans, dtype=jnp.int32)
    inverse = jnp.sum(
        jnp.where(targets[:, :, None] == member[None, None, :], member[None, :, None], 0), axis=1
    )
    right_at = inverse.T.reshape(-1).astype(jnp.int32)
    flags = (jnp.take(column, links, axis=0) == own_links[None, :]).astype(jnp.int32)
    flags = flags.reshape(groups, 2, spans)
    kept = jnp.stack([jnp.take(flags[:, e], inverse[e], axis=1) for e in range(2)], axis=-1)
    kept = kept.transpose(1, 0, 2).reshape(-1)
    by_group = (column - group * spans).reshape(groups, spans)
    left_at = jnp.sum(
        jnp.where(by_group[:, :, None] == member[None, None, :], member[None, :, None], 0), axis=1
    )
    left_at = left_at.T.reshape(-1).astype(jnp.int32)

    scale = 1.0 / math.sqrt(groups * block)
    squared, square_pairs = product(left_at, right_at, kept, left, right, None, scale)
    left = lax.all_gather(square_pairs, "row", axis=0, tiled=False)
    (updated,) = product(left_at, right_at, kept, left, right, own, scale)
    return (squared, updated)


def solution(mesh):
    in_specs = (P("col", "row"), P(None, "col"))
    out_specs = (P("col", "row"), P("col", "row"))
    return jax.shard_map(
        per_device, mesh=mesh, in_specs=in_specs, out_specs=out_specs, check_vma=False
    )
```

```python
import math

import jax
import jax.numpy as jnp
from jax import lax
from jax.experimental import pallas as pl
from jax.experimental.pallas import tpu as pltpu
from jax.sharding import PartitionSpec as P

SHARES = (1.0,)
TURNS = (0, -1, 1, 2)
CORES = 2
SIDE = 4
DIGIT = 32
CHUNK = 16
WEIGHT = 48
ROWS = 16
MIB = 1024 * 1024


def cuts(start, size):
    edges = [start]
    for i in range(len(SHARES)):
        edges.append(start + round(size * sum(SHARES[: i + 1]) / sum(SHARES)))
    return [(a, b - a) for a, b in zip(edges[:-1], edges[1:])]


def pair_columns(values, links, spans, halves):
    block = values.shape[0]
    lanes = 2 * block

    def body(flat_ref, links_ref, whole_ref, *half_refs):
        for (start, size), ref in zip(halves, half_refs):
            for m in range(start, start + size):
                first = flat_ref[:, m * block : (m + 1) * block]
                second = flat_ref[:, (spans + m) * block : (spans + m + 1) * block]
                both = jnp.concatenate([first, second], axis=1)
                whole_ref[m] = both
                ref[m - start] = both
        row = lax.broadcasted_iota(jnp.int32, (block, lanes), 0)
        numbers = jnp.broadcast_to(links_ref[...], (block, lanes))
        digits = jnp.where(row == 0, numbers // DIGIT, numbers % DIGIT)
        half_refs[0][halves[0][1]] = digits.astype(jnp.float32).astype(values.dtype)

    sizes = [spans, halves[0][1] + 1, halves[1][1]]
    padded = jnp.pad(links, (0, lanes - links.shape[0])).reshape(1, lanes)
    return pl.pallas_call(
        body,
        out_shape=[jax.ShapeDtypeStruct((size, block, lanes), values.dtype) for size in sizes],
        compiler_params=pltpu.CompilerParams(vmem_limit_bytes=16 * MIB),
    )(values, padded)


def join_columns(pick, flat_ref, spans, block):
    for m in range(spans):
        both = pick(m)
        flat_ref[:, m * block : (m + 1) * block] = both[:, :block]
        flat_ref[:, (spans + m) * block : (spans + m + 1) * block] = both[:, block:]


def sent_row(array, turn, swap):
    chips = lax.axis_size("row") // CORES
    order = [
        (x * CORES + c, ((x - turn) % chips) * CORES + (c + swap) % CORES)
        for x in range(chips)
        for c in range(CORES)
    ]
    return lax.ppermute(array, "row", order)


def sent_col(array, turn, axis):
    step = (turn, 0) if axis == 0 else (0, turn)
    order = [
        (z * SIDE + y, ((z - step[0]) % SIDE) * SIDE + (y - step[1]) % SIDE)
        for z in range(SIDE)
        for y in range(SIDE)
    ]
    return lax.ppermute(array, "col", order)


def ring(array, sent):
    size = array.shape[0]
    half = (size + 1) // 2
    behind, ahead = sent(array, -1), sent(array, 1)
    low = sent(lax.slice_in_dim(ahead, 0, half, axis=0), 1)
    high = sent(lax.slice_in_dim(behind, half, size, axis=0), -1)
    return [(array, 0, 0), (behind, 1, 0), (ahead, 2, 0), (low, 3, 0), (high, 3, half)]


def col_ring(array, axis):
    return ring(array, lambda x, turn: sent_col(x, turn, axis))


def row_slab(array, strips):
    near = ring(array, lambda x, turn: sent_row(x, turn, 0))
    slab = []
    for piece, turn, begin in near:
        end, at, ranges = begin + piece.shape[0], 0, []
        for start, size in strips:
            low, high = max(at, begin), min(at + size, end)
            if low < high:
                ranges.append((low - begin, start + low - at, high - low))
            at += size
        slab.append((piece, turn * CORES, ranges))
        slab.append((sent_row(piece, 0, 1), turn * CORES + 1, ranges))
    return slab


def taken(line, ranges):
    pieces = [lax.slice_in_dim(x, start, start + size, axis=0) for x in line for start, size in ranges]
    return jnp.concatenate(pieces, axis=0)


def slab_copies(refs, slab, rows_ref, left_ref, sems):
    copies = []
    for ref, (_, place, ranges) in zip(refs, slab):
        for offset, start, size in ranges:
            source = ref.at[pl.ds(offset, size)]
            target = left_ref.at[rows_ref[place], pl.ds(start, size)]
            copies.append(pltpu.make_async_copy(source, target, sems.at[len(copies)]))
    return copies


def panel_copies(refs, panels, starts, strips, more, groups_ref, right_ref, sems):
    runs, used = [], 0
    for strip, (refs_here, (pieces, axis), at, (member, size)) in enumerate(zip(refs, panels, starts, strips)):
        stride = size + (more if strip == 0 else 0)
        for a in range(0, size, CHUNK):
            some = min(CHUNK, size - a)
            copies = []
            for ref, (array, second, begin) in zip(refs_here, pieces):
                for first in range(SIDE):
                    offset = first * stride - begin
                    if 0 <= offset < array.shape[0]:
                        slot = first * SIDE + second if axis == 0 else second * SIDE + first
                        source = ref.at[pl.ds(offset + a, some)]
                        target = right_ref.at[groups_ref[slot], pl.ds(at + a, some)]
                        copies.append(pltpu.make_async_copy(source, target, sems.at[used]))
                        used += 1
            runs.append((copies, member + a, at + a, some))
    return runs


def panel_moves(strips):
    return SIDE * SIDE * sum(-(-size // CHUNK) for _, size in strips)


def block_sums(table_ref, left_ref, right_ref, spans, finish):
    positions = left_ref.shape[0]
    groups, _, block, lanes = right_ref.shape
    low = lax.broadcasted_iota(jnp.int32, (block, lanes), 1) < block

    def strip_of(member, e):
        row = e * spans + member
        return jnp.concatenate(
            [
                jnp.where(low, left_ref[j, table_ref[2 * j, row]], left_ref[j, table_ref[2 * j + 1, row]])
                for j in range(positions)
            ],
            axis=1,
        )

    def members(first, at, number):
        rows = [strip_of(first + u, e) for u in range(number) for e in range(2)]
        columns = [right_ref[:, at + u].reshape(groups * block, lanes) for u in range(number)]
        sums = jnp.dot(
            jnp.concatenate(rows, axis=0),
            jnp.concatenate(columns, axis=1),
            preferred_element_type=jnp.float32,
        )
        for u in range(number):
            across = slice(u * lanes, (u + 1) * lanes)
            top = 2 * u * block
            upper, lower = sums[top : top + block, across], sums[top + block : top + 2 * block, across]
            finish(first + u, at + u, jnp.where(low, upper, lower))

    def run(first, at, size):
        def step(t, carry):
            members(first + 4 * t, at + 4 * t, 2)
            members(first + 4 * t + 2, at + 4 * t + 2, 2)
            return carry

        lax.fori_loop(0, size // 4, step, 0)
        rest = size // 4 * 4
        if size - rest >= 2:
            members(first + rest, at + rest, 2)
        if size % 2:
            members(first + size - 1, at + size - 1, 1)

    return run


def first_product(table, expected, rows_at, groups_at, slab, panels, strips, spans, scale):
    positions = SIDE * CORES
    groups = 2 * positions
    block, lanes = slab[0][0].shape[-2:]
    starts = [sum(size for _, size in strips[:i]) for i in range(len(strips))]
    count = sum(size for _, size in strips)
    make = table is None
    left_moves = sum(len(ranges) for _, _, ranges in slab)

    def body(rows_ref, groups_ref, *refs):
        refs = list(refs)
        if make:
            expected_ref = refs.pop(0)
        else:
            table_ref = refs.pop(0)
        slab_refs = [refs.pop(0) for _ in slab]
        piece_refs = [[refs.pop(0) for _ in pieces] for pieces, _ in panels]
        done_ref = refs.pop(0)
        if make:
            table_out, left_ref, left_sem, right_ref, right_sem, table_ref, extra_ref, extra_sem, table_sem = refs
        else:
            left_ref, left_sem, right_ref, right_sem = refs

        runs = panel_copies(piece_refs, panels, starts, strips, int(make), groups_ref, right_ref, right_sem)
        extra_copies = []
        if make:
            (pieces, axis), size = panels[0], strips[0][1]
            for ref, (array, second, begin) in zip(piece_refs[0], pieces):
                for first in range(SIDE):
                    offset = first * (size + 1) - begin
                    if 0 <= offset < array.shape[0]:
                        slot = first * SIDE + second if axis == 0 else second * SIDE + first
                        source = ref.at[offset + size, pl.ds(0, ROWS)]
                        target = extra_ref.at[groups_ref[slot]]
                        sem = extra_sem.at[len(extra_copies)]
                        extra_copies.append(pltpu.make_async_copy(source, target, sem))
        left_copies = slab_copies(slab_refs, slab, rows_ref, left_ref, left_sem)
        for copy in extra_copies + left_copies + runs[0][0]:
            copy.start()
        left_ref[:, spans] = jnp.zeros((positions, block, lanes), left_ref.dtype)
        if make:
            for copy in extra_copies:
                copy.wait()
            row = lax.broadcasted_iota(jnp.int32, (groups, ROWS, lanes), 1)
            weights = jnp.where(row == 0, DIGIT, jnp.where(row == 1, 1, 0)).astype(jnp.float32)
            links = jnp.sum(extra_ref[...].astype(jnp.float32) * weights, axis=1).astype(jnp.int32)
            wanted = expected_ref[...]
            first_of = spans * lax.broadcasted_iota(jnp.int32, (groups, lanes), 0)
            table_out[...] = jnp.where(links == wanted, wanted - first_of, spans)
            copy = pltpu.make_async_copy(table_out, table_ref, table_sem)
            copy.start()
            copy.wait()
        for copy in left_copies:
            copy.wait()
        for copies, _, _, _ in runs[1:]:
            for copy in copies:
                copy.start()

        def finish(member, at, sums):
            done_ref[at] = (sums * scale).astype(done_ref.dtype)

        run = block_sums(table_ref, left_ref, right_ref, spans, finish)
        for copies, first, at, size in runs:
            for copy in copies:
                copy.wait()
            run(first, at, size)

    anywhere = pl.BlockSpec(memory_space=pl.ANY)
    in_vmem = pl.BlockSpec(memory_space=pltpu.VMEM)
    in_smem = pl.BlockSpec(memory_space=pltpu.SMEM)
    operands = [array for array, _, _ in slab] + [x for pieces, _ in panels for x, _, _ in pieces]
    flops = WEIGHT * count * block * lanes * groups * block
    cost = pl.CostEstimate(flops=flops, bytes_accessed=2 * sum(x.size for x in operands), transcendentals=0)
    in_specs = [in_smem, in_smem, in_vmem if make else in_smem] + [anywhere] * len(operands)
    out_shape = [jax.ShapeDtypeStruct((count, block, lanes), jnp.bfloat16)]
    scratch = [
        pltpu.VMEM((positions, spans + 1, block, lanes), jnp.bfloat16),
        pltpu.SemaphoreType.DMA((left_moves,)),
        pltpu.VMEM((groups, count, block, lanes), jnp.bfloat16),
        pltpu.SemaphoreType.DMA((panel_moves(strips),)),
    ]
    if make:
        out_shape.append(jax.ShapeDtypeStruct((groups, lanes), jnp.int32))
        scratch += [
            pltpu.SMEM((groups, lanes), jnp.int32),
            pltpu.VMEM((groups, ROWS, lanes), jnp.bfloat16),
            pltpu.SemaphoreType.DMA((groups,)),
            pltpu.SemaphoreType.DMA,
        ]
    out = pl.pallas_call(
        body,
        in_specs=in_specs,
        out_specs=[in_vmem] * len(out_shape),
        out_shape=out_shape,
        scratch_shapes=scratch,
        compiler_params=pltpu.CompilerParams(vmem_limit_bytes=60 * MIB),
        cost_estimate=cost,
    )(rows_at, groups_at, expected if make else table, *operands)
    return out if make else (*out, table)


def second_product(table, rows_at, groups_at, slab, panels, strips, spans, scale, square, own):
    positions = SIDE * CORES
    groups = 2 * positions
    block, lanes = own.shape[-2:]
    left_moves = sum(len(ranges) for _, _, ranges in slab)
    members, flat_strips = {}, []
    for part, part_strips in enumerate(strips):
        inside = 0
        for first, size in part_strips:
            at = sum(size for _, size in flat_strips)
            members.update({first + m: (part, inside + m, at + m) for m in range(size)})
            flat_strips.append((first, size))
            inside += size
    starts = [sum(size for _, size in flat_strips[:i]) for i in range(len(flat_strips))]

    def body(table_ref, rows_ref, groups_ref, *refs):
        refs = list(refs)
        slab_refs = [refs.pop(0) for _ in slab]
        piece_refs = [[refs.pop(0) for _ in pieces] for pieces, _ in panels]
        square_refs = [refs.pop(0) for _ in square]
        own_ref, square_ref, flat_ref, left_ref, left_sem, right_ref, right_sem, done_ref = refs
        left_copies = slab_copies(slab_refs, slab, rows_ref, left_ref, left_sem)
        runs = panel_copies(piece_refs, panels, starts, flat_strips, 1, groups_ref, right_ref, right_sem)
        for copy in left_copies + runs[0][0]:
            copy.start()
        left_ref[:, spans] = jnp.zeros((positions, block, lanes), left_ref.dtype)
        join_columns(lambda m: square_refs[members[m][0]][members[m][1]], square_ref, spans, block)
        for copy in left_copies:
            copy.wait()
        for copies, _, _, _ in runs[1:]:
            for copy in copies:
                copy.start()

        def finish(member, at, sums):
            own_part = 1.5 * own_ref[member].astype(jnp.float32)
            done_ref[at] = (own_part - (0.5 * scale) * sums).astype(done_ref.dtype)

        run = block_sums(table_ref, left_ref, right_ref, spans, finish)
        for copies, first, at, size in runs:
            for copy in copies:
                copy.wait()
            run(first, at, size)
        join_columns(lambda m: done_ref[members[m][2]], flat_ref, spans, block)

    anywhere = pl.BlockSpec(memory_space=pl.ANY)
    in_vmem = pl.BlockSpec(memory_space=pltpu.VMEM)
    in_smem = pl.BlockSpec(memory_space=pltpu.SMEM)
    operands = [array for array, _, _ in slab] + [x for pieces, _ in panels for x, _, _ in pieces]
    flops = WEIGHT * spans * block * lanes * groups * block
    cost = pl.CostEstimate(flops=flops, bytes_accessed=2 * sum(x.size for x in operands), transcendentals=0)
    flat = jax.ShapeDtypeStruct((block, spans * lanes), jnp.bfloat16)
    return pl.pallas_call(
        body,
        in_specs=[in_smem] * 3 + [anywhere] * len(operands) + [in_vmem] * (len(square) + 1),
        out_specs=[in_vmem] * 2,
        out_shape=[flat] * 2,
        scratch_shapes=[
            pltpu.VMEM((positions, spans + 1, block, lanes), jnp.bfloat16),
            pltpu.SemaphoreType.DMA((left_moves,)),
            pltpu.VMEM((groups, spans, block, lanes), jnp.bfloat16),
            pltpu.SemaphoreType.DMA((panel_moves(flat_strips),)),
            pltpu.VMEM((spans, block, lanes), jnp.bfloat16),
        ],
        compiler_params=pltpu.CompilerParams(vmem_limit_bytes=60 * MIB),
        cost_estimate=cost,
    )(table, rows_at, groups_at, *operands, *square, own)


def per_device(values, pattern):
    block = values.shape[0]
    rows_here = values.shape[1] // block
    groups = lax.axis_size("col")
    spans = pattern.shape[0] // groups
    mine, group = lax.axis_index("row"), lax.axis_index("col")
    z, y = group // SIDE, group % SIDE
    column = pattern[:, 0]
    scale = 1.0 / math.sqrt(groups * block)

    split = (spans + 1) // 2
    halves = [(0, split), (split, spans - split)]
    own_links = lax.dynamic_slice_in_dim(column, mine * rows_here, rows_here, 0)
    own, *pieces = pair_columns(values, own_links, spans, halves)
    lines = []
    for axis, piece in enumerate(pieces):
        *three, (low, _, _), (high, _, _) = col_ring(piece, axis)
        lines.append([x for x, _, _ in three] + [jnp.concatenate([low, high], axis=0)])
    lines = lax.optimization_barrier(lines)
    first_slab = row_slab(own, [(0, spans)])

    chip, core = mine // CORES, mine % CORES
    rows_at = [((chip + t) % SIDE) * CORES + (core + swap) % CORES for t in TURNS for swap in range(CORES)]
    groups_at = [((z + t) % SIDE) * SIDE + (y + u) % SIDE for t in TURNS for u in TURNS]
    rows_at = jnp.stack(rows_at).astype(jnp.int32)
    groups_at = jnp.stack(groups_at).astype(jnp.int32)
    member = jnp.arange(spans, dtype=jnp.int32)
    found = column.reshape(groups, spans, 1) == own_links[None, None, :]
    expected = jnp.sum(jnp.where(found, member[None, :, None], 0), axis=1)
    expected = expected + spans * jnp.arange(groups, dtype=jnp.int32)[:, None]
    expected = jnp.pad(expected, ((0, 0), (0, 2 * block - rows_here)), constant_values=-1)

    half_cuts = [cuts(start, size) for start, size in halves]
    all_strips, planes = [], []
    for part in range(len(SHARES)):
        strips = [half_cuts[axis][part] for axis in range(2)]
        loads = []
        for axis, (start, size) in enumerate(strips):
            ranges = [(start - halves[axis][0], size)]
            if part == 0 and axis == 0:
                ranges.append((split, 1))
            loads.append(taken(lines[axis], ranges))
        if part:
            loads, planes[-1] = lax.optimization_barrier((loads, planes[-1]))
        planes.append([col_ring(load, 1 - axis) for axis, load in enumerate(loads)])
        all_strips.append(strips)

    table = None
    second_slab, panels, squares = [], [], []
    for plane, strips in zip(planes, all_strips):
        legs = [(ring_pieces, axis) for axis, ring_pieces in enumerate(plane)]
        square, table = first_product(
            table, expected, rows_at, groups_at, first_slab, legs, strips, spans, scale
        )
        second_slab += row_slab(square, strips)
        panels += legs
        squares.append(square)
    where = (table, rows_at, groups_at)
    return tuple(second_product(*where, second_slab, panels, all_strips, spans, scale, squares, own))


def solution(mesh):
    in_specs = (P("col", "row"), P(None, "col"))
    out_specs = (P("col", "row"), P("col", "row"))
    return jax.shard_map(
        per_device, mesh=mesh, in_specs=in_specs, out_specs=out_specs, check_vma=False
    )
```

```python
import math

import jax
import jax.numpy as jnp
from jax import lax
from jax.experimental import pallas as pl
from jax.experimental.pallas import tpu as pltpu
from jax.sharding import PartitionSpec as P

TURNS = (0, -1, 1, 2)
CORES = 2
SIDE = 4
DIGIT = 32
CHUNK = 12
STEP = 6
WEIGHT = 48
ROWS = 16
MIB = 1024 * 1024


def pair_columns(values, links, spans, halves):
    block = values.shape[0]
    lanes = 2 * block

    def body(flat_ref, links_ref, whole_ref, *half_refs):
        for (start, size), ref in zip(halves, half_refs):
            for m in range(start, start + size):
                first = flat_ref[:, m * block : (m + 1) * block]
                second = flat_ref[:, (spans + m) * block : (spans + m + 1) * block]
                both = jnp.concatenate([first, second], axis=1)
                whole_ref[m] = both
                ref[m - start] = both
        row = lax.broadcasted_iota(jnp.int32, (block, lanes), 0)
        numbers = jnp.broadcast_to(links_ref[...], (block, lanes))
        digits = jnp.where(row == 0, numbers // DIGIT, numbers % DIGIT)
        half_refs[0][halves[0][1]] = digits.astype(jnp.float32).astype(values.dtype)

    sizes = [spans, halves[0][1] + 1, halves[1][1]]
    padded = jnp.pad(links, (0, lanes - links.shape[0])).reshape(1, lanes)
    return pl.pallas_call(
        body,
        out_shape=[jax.ShapeDtypeStruct((size, block, lanes), values.dtype) for size in sizes],
        compiler_params=pltpu.CompilerParams(vmem_limit_bytes=16 * MIB),
    )(values, padded)


def join_columns(pick, flat_ref, spans, block):
    for m in range(spans):
        both = pick(m)
        flat_ref[:, m * block : (m + 1) * block] = both[:, :block]
        flat_ref[:, (spans + m) * block : (spans + m + 1) * block] = both[:, block:]


def sent_row(array, turn, swap):
    chips = lax.axis_size("row") // CORES
    order = [
        (x * CORES + c, ((x - turn) % chips) * CORES + (c + swap) % CORES)
        for x in range(chips)
        for c in range(CORES)
    ]
    return lax.ppermute(array, "row", order)


def sent_col(array, turn, axis):
    step = (turn, 0) if axis == 0 else (0, turn)
    order = [
        (z * SIDE + y, ((z - step[0]) % SIDE) * SIDE + (y - step[1]) % SIDE)
        for z in range(SIDE)
        for y in range(SIDE)
    ]
    return lax.ppermute(array, "col", order)


def ring(array, sent, nearest=None):
    size = array.shape[0]
    half = (size + 1) // 2
    behind, ahead = nearest or (sent(array, -1), sent(array, 1))
    low = sent(lax.slice_in_dim(ahead, 0, half, axis=0), 1)
    high = sent(lax.slice_in_dim(behind, half, size, axis=0), -1)
    return [(array, 0, 0), (behind, 1, 0), (ahead, 2, 0), (low, 3, 0), (high, 3, half)]


def col_ring(array, axis):
    return ring(array, lambda x, turn: sent_col(x, turn, axis))


def row_slab(array, strips):
    behind, ahead, swapped = sent_row(array, -1, 0), sent_row(array, 1, 0), sent_row(array, 0, 1)
    nearest = lax.optimization_barrier((behind, ahead, swapped))
    near = ring(array, lambda x, turn: sent_row(x, turn, 0), nearest[:2])
    slab = []
    for piece, turn, begin in near:
        end, at, ranges = begin + piece.shape[0], 0, []
        for start, size in strips:
            low, high = max(at, begin), min(at + size, end)
            if low < high:
                ranges.append((low - begin, start + low - at, high - low))
            at += size
        slab.append((piece, turn * CORES, ranges))
        other = nearest[2] if turn == 0 else sent_row(piece, 0, 1)
        slab.append((other, turn * CORES + 1, ranges))
    return slab


def swapped_slab(chips):
    size = chips[0].shape[0]
    swapped = sent_row(jnp.concatenate(chips, axis=0), 0, 1)
    slab = []
    for step, x in enumerate(chips):
        place = CORES * TURNS.index((step + 1) % SIDE - 1)
        slab += [(x, place, [(0, 0, size)]), (swapped, place + 1, [(step * size, 0, size)])]
    return slab


def slab_copies(refs, slab, rows_ref, left_ref, sems):
    copies = []
    for ref, (_, place, ranges) in zip(refs, slab):
        for offset, start, size in ranges:
            source = ref.at[pl.ds(offset, size)]
            target = left_ref.at[rows_ref[place], pl.ds(start, size)]
            copies.append(pltpu.make_async_copy(source, target, sems.at[len(copies)]))
    return copies


def pieces_of(size, strip):
    edges = list(range(STEP if strip == 0 else 0, size, CHUNK))
    edges = sorted({0, *edges, size})
    return [(a, b - a) for a, b in zip(edges[:-1], edges[1:])]


def panel_copies(refs, panels, starts, strips, more, groups_ref, right_ref, sems):
    runs, used = [], 0
    for strip, (refs_here, (pieces, axis), at, (member, size)) in enumerate(zip(refs, panels, starts, strips)):
        stride = size + (more if strip == 0 else 0)
        for a, some in pieces_of(size, strip):
            copies = []
            for ref, (array, second, begin) in zip(refs_here, pieces):
                for first in range(SIDE):
                    offset = first * stride - begin
                    if 0 <= offset < array.shape[0]:
                        slot = first * SIDE + second if axis == 0 else second * SIDE + first
                        source = ref.at[pl.ds(offset + a, some)]
                        target = right_ref.at[groups_ref[slot], pl.ds(at + a, some)]
                        copies.append(pltpu.make_async_copy(source, target, sems.at[used]))
                        used += 1
            runs.append((copies, member + a, at + a, some))
    return runs


def panel_moves(strips):
    return SIDE * SIDE * sum(len(pieces_of(size, i)) for i, (_, size) in enumerate(strips))


def block_sums(table_ref, left_ref, right_ref, spans, finish):
    positions = left_ref.shape[0]
    groups, _, block, lanes = right_ref.shape
    low = lax.broadcasted_iota(jnp.int32, (block, lanes), 1) < block

    def strip_of(member, e):
        row = e * spans + member
        return jnp.concatenate(
            [
                jnp.where(low, left_ref[j, table_ref[2 * j, row]], left_ref[j, table_ref[2 * j + 1, row]])
                for j in range(positions)
            ],
            axis=1,
        )

    def members(first, at, number):
        rows = [strip_of(first + u, e) for u in range(number) for e in range(2)]
        columns = [right_ref[:, at + u].reshape(groups * block, lanes) for u in range(number)]
        sums = jnp.dot(
            jnp.concatenate(rows, axis=0),
            jnp.concatenate(columns, axis=1),
            preferred_element_type=jnp.float32,
        )
        for u in range(number):
            across = slice(u * lanes, (u + 1) * lanes)
            top = 2 * u * block
            upper, lower = sums[top : top + block, across], sums[top + block : top + 2 * block, across]
            finish(first + u, at + u, jnp.where(low, upper, lower))

    def run(first, at, size):
        def step(t, carry):
            for u in range(0, STEP, 2):
                members(first + STEP * t + u, at + STEP * t + u, 2)
            return carry

        lax.fori_loop(0, size // STEP, step, 0)
        for u in range(size // STEP * STEP, size - 1, 2):
            members(first + u, at + u, 2)
        if size % 2:
            members(first + size - 1, at + size - 1, 1)

    return run


def first_product(table, expected, rows_at, groups_at, slab, panels, strips, spans, scale):
    positions = SIDE * CORES
    groups = 2 * positions
    block, lanes = slab[0][0].shape[-2:]
    starts = [sum(size for _, size in strips[:i]) for i in range(len(strips))]
    count = sum(size for _, size in strips)
    make = table is None
    left_moves = sum(len(ranges) for _, _, ranges in slab)

    def body(rows_ref, groups_ref, *refs):
        refs = list(refs)
        if make:
            expected_ref = refs.pop(0)
        else:
            table_ref = refs.pop(0)
        slab_refs = [refs.pop(0) for _ in slab]
        piece_refs = [[refs.pop(0) for _ in pieces] for pieces, _ in panels]
        done_ref = refs.pop(0)
        if make:
            table_out, left_ref, left_sem, right_ref, right_sem, table_ref, extra_ref, extra_sem, table_sem = refs
        else:
            left_ref, left_sem, right_ref, right_sem = refs

        runs = panel_copies(piece_refs, panels, starts, strips, int(make), groups_ref, right_ref, right_sem)
        extra_copies = []
        if make:
            (pieces, axis), size = panels[0], strips[0][1]
            for ref, (array, second, begin) in zip(piece_refs[0], pieces):
                for first in range(SIDE):
                    offset = first * (size + 1) - begin
                    if 0 <= offset < array.shape[0]:
                        slot = first * SIDE + second if axis == 0 else second * SIDE + first
                        source = ref.at[offset + size, pl.ds(0, ROWS)]
                        target = extra_ref.at[groups_ref[slot]]
                        sem = extra_sem.at[len(extra_copies)]
                        extra_copies.append(pltpu.make_async_copy(source, target, sem))
        left_copies = slab_copies(slab_refs, slab, rows_ref, left_ref, left_sem)
        for copy in extra_copies + left_copies + runs[0][0]:
            copy.start()
        left_ref[:, spans] = jnp.zeros((positions, block, lanes), left_ref.dtype)
        if make:
            for copy in extra_copies:
                copy.wait()
            row = lax.broadcasted_iota(jnp.int32, (groups, ROWS, lanes), 1)
            weights = jnp.where(row == 0, DIGIT, jnp.where(row == 1, 1, 0)).astype(jnp.float32)
            links = jnp.sum(extra_ref[...].astype(jnp.float32) * weights, axis=1).astype(jnp.int32)
            wanted = expected_ref[...]
            first_of = spans * lax.broadcasted_iota(jnp.int32, (groups, lanes), 0)
            table_out[...] = jnp.where(links == wanted, wanted - first_of, spans)
            copy = pltpu.make_async_copy(table_out, table_ref, table_sem)
            copy.start()
            copy.wait()
        for copy in left_copies:
            copy.wait()
        for copies, _, _, _ in runs[1:]:
            for copy in copies:
                copy.start()

        def finish(member, at, sums):
            done_ref[at] = (sums * scale).astype(done_ref.dtype)

        run = block_sums(table_ref, left_ref, right_ref, spans, finish)
        for copies, first, at, size in runs:
            for copy in copies:
                copy.wait()
            run(first, at, size)

    anywhere = pl.BlockSpec(memory_space=pl.ANY)
    in_vmem = pl.BlockSpec(memory_space=pltpu.VMEM)
    in_smem = pl.BlockSpec(memory_space=pltpu.SMEM)
    operands = [array for array, _, _ in slab] + [x for pieces, _ in panels for x, _, _ in pieces]
    flops = WEIGHT * count * block * lanes * groups * block
    cost = pl.CostEstimate(flops=flops, bytes_accessed=2 * sum(x.size for x in operands), transcendentals=0)
    in_specs = [in_smem, in_smem, in_vmem if make else in_smem] + [anywhere] * len(operands)
    out_shape = [jax.ShapeDtypeStruct((count, block, lanes), jnp.bfloat16)]
    scratch = [
        pltpu.VMEM((positions, spans + 1, block, lanes), jnp.bfloat16),
        pltpu.SemaphoreType.DMA((left_moves,)),
        pltpu.VMEM((groups, count, block, lanes), jnp.bfloat16),
        pltpu.SemaphoreType.DMA((panel_moves(strips),)),
    ]
    if make:
        out_shape.append(jax.ShapeDtypeStruct((groups, lanes), jnp.int32))
        scratch += [
            pltpu.SMEM((groups, lanes), jnp.int32),
            pltpu.VMEM((groups, ROWS, lanes), jnp.bfloat16),
            pltpu.SemaphoreType.DMA((groups,)),
            pltpu.SemaphoreType.DMA,
        ]
    out = pl.pallas_call(
        body,
        in_specs=in_specs,
        out_specs=[in_vmem] * len(out_shape),
        out_shape=out_shape,
        scratch_shapes=scratch,
        compiler_params=pltpu.CompilerParams(vmem_limit_bytes=60 * MIB),
        cost_estimate=cost,
    )(rows_at, groups_at, expected if make else table, *operands)
    return out if make else (*out, table)


def second_product(table, rows_at, groups_at, slab, panels, strips, spans, scale, square, own):
    positions = SIDE * CORES
    groups = 2 * positions
    block, lanes = own.shape[-2:]
    left_moves = sum(len(ranges) for _, _, ranges in slab)
    members, flat_strips = {}, []
    for part, part_strips in enumerate(strips):
        inside = 0
        for first, size in part_strips:
            at = sum(size for _, size in flat_strips)
            members.update({first + m: (part, inside + m, at + m) for m in range(size)})
            flat_strips.append((first, size))
            inside += size
    starts = [sum(size for _, size in flat_strips[:i]) for i in range(len(flat_strips))]

    def body(table_ref, rows_ref, groups_ref, *refs):
        refs = list(refs)
        slab_refs = [refs.pop(0) for _ in slab]
        piece_refs = [[refs.pop(0) for _ in pieces] for pieces, _ in panels]
        square_refs = [refs.pop(0) for _ in square]
        own_ref, square_ref, flat_ref, left_ref, left_sem, right_ref, right_sem, done_ref = refs
        left_copies = slab_copies(slab_refs, slab, rows_ref, left_ref, left_sem)
        runs = panel_copies(piece_refs, panels, starts, flat_strips, 1, groups_ref, right_ref, right_sem)
        for copy in left_copies + runs[0][0]:
            copy.start()
        left_ref[:, spans] = jnp.zeros((positions, block, lanes), left_ref.dtype)
        join_columns(lambda m: square_refs[members[m][0]][members[m][1]], square_ref, spans, block)
        for copy in left_copies:
            copy.wait()
        for copies, _, _, _ in runs[1:]:
            for copy in copies:
                copy.start()

        def finish(member, at, sums):
            own_part = 1.5 * own_ref[member].astype(jnp.float32)
            done_ref[at] = (own_part - (0.5 * scale) * sums).astype(done_ref.dtype)

        run = block_sums(table_ref, left_ref, right_ref, spans, finish)
        for copies, first, at, size in runs:
            for copy in copies:
                copy.wait()
            run(first, at, size)
        join_columns(lambda m: done_ref[members[m][2]], flat_ref, spans, block)

    anywhere = pl.BlockSpec(memory_space=pl.ANY)
    in_vmem = pl.BlockSpec(memory_space=pltpu.VMEM)
    in_smem = pl.BlockSpec(memory_space=pltpu.SMEM)
    operands = [array for array, _, _ in slab] + [x for pieces, _ in panels for x, _, _ in pieces]
    flops = WEIGHT * spans * block * lanes * groups * block
    cost = pl.CostEstimate(flops=flops, bytes_accessed=2 * sum(x.size for x in operands), transcendentals=0)
    flat = jax.ShapeDtypeStruct((block, spans * lanes), jnp.bfloat16)
    return pl.pallas_call(
        body,
        in_specs=[in_smem] * 3 + [anywhere] * len(operands) + [in_vmem] * (len(square) + 1),
        out_specs=[in_vmem] * 2,
        out_shape=[flat] * 2,
        scratch_shapes=[
            pltpu.VMEM((positions, spans + 1, block, lanes), jnp.bfloat16),
            pltpu.SemaphoreType.DMA((left_moves,)),
            pltpu.VMEM((groups, spans, block, lanes), jnp.bfloat16),
            pltpu.SemaphoreType.DMA((panel_moves(flat_strips),)),
            pltpu.VMEM((spans, block, lanes), jnp.bfloat16),
        ],
        compiler_params=pltpu.CompilerParams(vmem_limit_bytes=60 * MIB),
        cost_estimate=cost,
    )(table, rows_at, groups_at, *operands, *square, own)


def per_device(values, pattern):
    block = values.shape[0]
    rows_here = values.shape[1] // block
    groups = lax.axis_size("col")
    spans = pattern.shape[0] // groups
    mine, group = lax.axis_index("row"), lax.axis_index("col")
    z, y = group // SIDE, group % SIDE
    column = pattern[:, 0]
    scale = 1.0 / math.sqrt(groups * block)

    split = (spans + 1) // 2
    halves = [(0, split), (split, spans - split)]
    own_links = lax.dynamic_slice_in_dim(column, mine * rows_here, rows_here, 0)
    own, *pieces = pair_columns(values, own_links, spans, halves)
    lines = []
    for axis, piece in enumerate(pieces):
        *three, (low, _, _), (high, _, _) = col_ring(piece, axis)
        lines.append([x for x, _, _ in three] + [jnp.concatenate([low, high], axis=0)])
    on_1 = sent_row(own, 1, 0)
    lines, on_1 = lax.optimization_barrier((lines, on_1))
    on_2 = sent_row(on_1, 1, 0)
    on_3 = sent_row(on_2, 1, 0)

    chip, core = mine // CORES, mine % CORES
    rows_at = [((chip + t) % SIDE) * CORES + (core + swap) % CORES for t in TURNS for swap in range(CORES)]
    groups_at = [((z + t) % SIDE) * SIDE + (y + u) % SIDE for t in TURNS for u in TURNS]
    rows_at = jnp.stack(rows_at).astype(jnp.int32)
    groups_at = jnp.stack(groups_at).astype(jnp.int32)
    member = jnp.arange(spans, dtype=jnp.int32)
    found = column.reshape(groups, spans, 1) == own_links[None, None, :]
    expected = jnp.sum(jnp.where(found, member[None, :, None], 0), axis=1)
    expected = expected + spans * jnp.arange(groups, dtype=jnp.int32)[:, None]
    expected = jnp.pad(expected, ((0, 0), (0, 2 * block - rows_here)), constant_values=-1)

    planes = [col_ring(jnp.concatenate(line, axis=0), 1 - axis) for axis, line in enumerate(lines)]
    nearest = [x for plane in planes for x, place, _ in plane if place in (1, 2)]
    chips, _ = lax.optimization_barrier(((own, on_1, on_2, on_3), nearest))
    first_slab = swapped_slab(chips)
    panels = [(plane, axis) for axis, plane in enumerate(planes)]
    square, table = first_product(
        None, expected, rows_at, groups_at, first_slab, panels, halves, spans, scale
    )
    second_slab = row_slab(square, halves)
    squares, all_strips = [square], [halves]
    where = (table, rows_at, groups_at)
    return tuple(second_product(*where, second_slab, panels, all_strips, spans, scale, squares, own))


def solution(mesh):
    in_specs = (P("col", "row"), P(None, "col"))
    out_specs = (P("col", "row"), P("col", "row"))
    return jax.shard_map(
        per_device, mesh=mesh, in_specs=in_specs, out_specs=out_specs, check_vma=False
    )
```

```python
import math

import jax
import jax.numpy as jnp
from jax import lax
from jax.experimental import pallas as pl
from jax.experimental.pallas import tpu as pltpu
from jax.sharding import PartitionSpec as P

TURNS = (0, -1, 1, 2)
CORES = 2
SIDE = 4
DIGIT = 32
CHUNK = 12
STEP = 6
WEIGHT = 48
ROWS = 16
MIB = 1024 * 1024


def pair_columns(values, links, spans, halves):
    block = values.shape[0]
    lanes = 2 * block

    def body(flat_ref, links_ref, whole_ref, *half_refs):
        for (start, size), ref in zip(halves, half_refs):
            for m in range(start, start + size):
                first = flat_ref[:, m * block : (m + 1) * block]
                second = flat_ref[:, (spans + m) * block : (spans + m + 1) * block]
                both = jnp.concatenate([first, second], axis=1)
                whole_ref[m] = both
                ref[m - start] = both
        row = lax.broadcasted_iota(jnp.int32, (block, lanes), 0)
        numbers = jnp.broadcast_to(links_ref[...], (block, lanes))
        digits = jnp.where(row == 0, numbers // DIGIT, numbers % DIGIT)
        half_refs[0][halves[0][1]] = digits.astype(jnp.float32).astype(values.dtype)

    sizes = [spans, halves[0][1] + 1, halves[1][1]]
    padded = jnp.pad(links, (0, lanes - links.shape[0])).reshape(1, lanes)
    return pl.pallas_call(
        body,
        out_shape=[jax.ShapeDtypeStruct((size, block, lanes), values.dtype) for size in sizes],
        compiler_params=pltpu.CompilerParams(vmem_limit_bytes=16 * MIB),
    )(values, padded)


def join_columns(pick, flat_ref, spans, block):
    for m in range(spans):
        both = pick(m)
        flat_ref[:, m * block : (m + 1) * block] = both[:, :block]
        flat_ref[:, (spans + m) * block : (spans + m + 1) * block] = both[:, block:]


def sent_row(array, turn, swap):
    chips = lax.axis_size("row") // CORES
    order = [
        (x * CORES + c, ((x - turn) % chips) * CORES + (c + swap) % CORES)
        for x in range(chips)
        for c in range(CORES)
    ]
    return lax.ppermute(array, "row", order)


def sent_col(array, turn, axis):
    step = (turn, 0) if axis == 0 else (0, turn)
    order = [
        (z * SIDE + y, ((z - step[0]) % SIDE) * SIDE + (y - step[1]) % SIDE)
        for z in range(SIDE)
        for y in range(SIDE)
    ]
    return lax.ppermute(array, "col", order)


def ring(array, sent, nearest=None):
    size = array.shape[0]
    half = (size + 1) // 2
    behind, ahead = nearest or (sent(array, -1), sent(array, 1))
    low = sent(lax.slice_in_dim(ahead, 0, half, axis=0), 1)
    high = sent(lax.slice_in_dim(behind, half, size, axis=0), -1)
    return [(array, 0, 0), (behind, 1, 0), (ahead, 2, 0), (low, 3, 0), (high, 3, half)]


def col_ring(array, axis):
    return ring(array, lambda x, turn: sent_col(x, turn, axis))


def row_slab(array, strips):
    behind, ahead, swapped = sent_row(array, -1, 0), sent_row(array, 1, 0), sent_row(array, 0, 1)
    nearest = lax.optimization_barrier((behind, ahead, swapped))
    near = ring(array, lambda x, turn: sent_row(x, turn, 0), nearest[:2])
    slab = []
    for piece, turn, begin in near:
        end, at, ranges = begin + piece.shape[0], 0, []
        for start, size in strips:
            low, high = max(at, begin), min(at + size, end)
            if low < high:
                ranges.append((low - begin, start + low - at, high - low))
            at += size
        slab.append((piece, turn * CORES, ranges))
        other = nearest[2] if turn == 0 else sent_row(piece, 0, 1)
        slab.append((other, turn * CORES + 1, ranges))
    return slab


def halves_slab(low, high, strips):
    ahead_low, behind_high = sent_row(low, 1, 0), sent_row(high, -1, 0)
    ahead_high, behind_low = sent_row(high, 1, 0), sent_row(low, -1, 0)
    far = (sent_row(ahead_low, 1, 0), sent_row(behind_high, -1, 0))
    slab = []
    chips = [(low, high), (behind_low, behind_high), (ahead_low, ahead_high), far]
    for turn, pair in enumerate(chips):
        for x, (start, size) in zip(pair, strips):
            slab.append((x, turn * CORES, [(0, start, size)]))
            slab.append((sent_row(x, 0, 1), turn * CORES + 1, [(0, start, size)]))
    return slab


def swapped_slab(chips):
    size = chips[0].shape[0]
    swapped = sent_row(jnp.concatenate(chips, axis=0), 0, 1)
    slab = []
    for step, x in enumerate(chips):
        place = CORES * TURNS.index((step + 1) % SIDE - 1)
        slab += [(x, place, [(0, 0, size)]), (swapped, place + 1, [(step * size, 0, size)])]
    return slab


def slab_copies(refs, slab, rows_ref, left_ref, sems):
    copies = []
    for ref, (_, place, ranges) in zip(refs, slab):
        for offset, start, size in ranges:
            source = ref.at[pl.ds(offset, size)]
            target = left_ref.at[rows_ref[place], pl.ds(start, size)]
            copies.append(pltpu.make_async_copy(source, target, sems.at[len(copies)]))
    return copies


def pieces_of(size, strip):
    edges = list(range(STEP if strip == 0 else 0, size, CHUNK))
    edges = sorted({0, *edges, size})
    return [(a, b - a) for a, b in zip(edges[:-1], edges[1:])]


def panel_copies(refs, panels, starts, strips, more, groups_ref, right_ref, sems):
    runs, used = [], 0
    for strip, (refs_here, (pieces, axis), at, (member, size)) in enumerate(zip(refs, panels, starts, strips)):
        stride = size + (more if strip == 0 else 0)
        for a, some in pieces_of(size, strip):
            copies = []
            for ref, (array, second, begin) in zip(refs_here, pieces):
                for first in range(SIDE):
                    offset = first * stride - begin
                    if 0 <= offset < array.shape[0]:
                        slot = first * SIDE + second if axis == 0 else second * SIDE + first
                        source = ref.at[pl.ds(offset + a, some)]
                        target = right_ref.at[groups_ref[slot], pl.ds(at + a, some)]
                        copies.append(pltpu.make_async_copy(source, target, sems.at[used]))
                        used += 1
            runs.append((copies, member + a, at + a, some))
    return runs


def panel_moves(strips):
    return SIDE * SIDE * sum(len(pieces_of(size, i)) for i, (_, size) in enumerate(strips))


def block_sums(table_ref, left_ref, right_ref, spans, finish):
    positions = left_ref.shape[0]
    groups, _, block, lanes = right_ref.shape
    low = lax.broadcasted_iota(jnp.int32, (block, lanes), 1) < block

    def strip_of(member, e):
        row = e * spans + member
        return jnp.concatenate(
            [
                jnp.where(low, left_ref[j, table_ref[2 * j, row]], left_ref[j, table_ref[2 * j + 1, row]])
                for j in range(positions)
            ],
            axis=1,
        )

    def members(first, at, number):
        rows = [strip_of(first + u, e) for u in range(number) for e in range(2)]
        columns = [right_ref[:, at + u].reshape(groups * block, lanes) for u in range(number)]
        sums = jnp.dot(
            jnp.concatenate(rows, axis=0),
            jnp.concatenate(columns, axis=1),
            preferred_element_type=jnp.float32,
        )
        for u in range(number):
            across = slice(u * lanes, (u + 1) * lanes)
            top = 2 * u * block
            upper, lower = sums[top : top + block, across], sums[top + block : top + 2 * block, across]
            finish(first + u, at + u, jnp.where(low, upper, lower))

    def run(first, at, size):
        def step(t, carry):
            for u in range(0, STEP, 2):
                members(first + STEP * t + u, at + STEP * t + u, 2)
            return carry

        lax.fori_loop(0, size // STEP, step, 0)
        for u in range(size // STEP * STEP, size - 1, 2):
            members(first + u, at + u, 2)
        if size % 2:
            members(first + size - 1, at + size - 1, 1)

    return run


def first_product(table, expected, rows_at, groups_at, slab, panels, strips, spans, scale):
    positions = SIDE * CORES
    groups = 2 * positions
    block, lanes = slab[0][0].shape[-2:]
    starts = [sum(size for _, size in strips[:i]) for i in range(len(strips))]
    count = sum(size for _, size in strips)
    make = table is None
    left_moves = sum(len(ranges) for _, _, ranges in slab)

    def body(rows_ref, groups_ref, *refs):
        refs = list(refs)
        if make:
            expected_ref = refs.pop(0)
        else:
            table_ref = refs.pop(0)
        slab_refs = [refs.pop(0) for _ in slab]
        piece_refs = [[refs.pop(0) for _ in pieces] for pieces, _ in panels]
        done_refs = [refs.pop(0) for _ in strips]
        if make:
            table_out, left_ref, left_sem, right_ref, right_sem, table_ref, extra_ref, extra_sem, table_sem = refs
        else:
            left_ref, left_sem, right_ref, right_sem = refs

        runs = panel_copies(piece_refs, panels, starts, strips, int(make), groups_ref, right_ref, right_sem)
        extra_copies = []
        if make:
            (pieces, axis), size = panels[0], strips[0][1]
            for ref, (array, second, begin) in zip(piece_refs[0], pieces):
                for first in range(SIDE):
                    offset = first * (size + 1) - begin
                    if 0 <= offset < array.shape[0]:
                        slot = first * SIDE + second if axis == 0 else second * SIDE + first
                        source = ref.at[offset + size, pl.ds(0, ROWS)]
                        target = extra_ref.at[groups_ref[slot]]
                        sem = extra_sem.at[len(extra_copies)]
                        extra_copies.append(pltpu.make_async_copy(source, target, sem))
        left_copies = slab_copies(slab_refs, slab, rows_ref, left_ref, left_sem)
        for copy in extra_copies + left_copies + runs[0][0]:
            copy.start()
        left_ref[:, spans] = jnp.zeros((positions, block, lanes), left_ref.dtype)
        if make:
            for copy in extra_copies:
                copy.wait()
            row = lax.broadcasted_iota(jnp.int32, (groups, ROWS, lanes), 1)
            weights = jnp.where(row == 0, DIGIT, jnp.where(row == 1, 1, 0)).astype(jnp.float32)
            links = jnp.sum(extra_ref[...].astype(jnp.float32) * weights, axis=1).astype(jnp.int32)
            wanted = expected_ref[...]
            first_of = spans * lax.broadcasted_iota(jnp.int32, (groups, lanes), 0)
            table_out[...] = jnp.where(links == wanted, wanted - first_of, spans)
            copy = pltpu.make_async_copy(table_out, table_ref, table_sem)
            copy.start()
            copy.wait()
        for copy in left_copies:
            copy.wait()
        for copies, _, _, _ in runs[1:]:
            for copy in copies:
                copy.start()

        for copies, first, at, size in runs:
            for copy in copies:
                copy.wait()
            strip = max(i for i, start in enumerate(starts) if start <= at)

            def finish(member, at, sums, done_ref=done_refs[strip], start=starts[strip]):
                done_ref[at - start] = (sums * scale).astype(done_ref.dtype)

            block_sums(table_ref, left_ref, right_ref, spans, finish)(first, at, size)

    anywhere = pl.BlockSpec(memory_space=pl.ANY)
    in_vmem = pl.BlockSpec(memory_space=pltpu.VMEM)
    in_smem = pl.BlockSpec(memory_space=pltpu.SMEM)
    operands = [array for array, _, _ in slab] + [x for pieces, _ in panels for x, _, _ in pieces]
    flops = WEIGHT * count * block * lanes * groups * block
    cost = pl.CostEstimate(flops=flops, bytes_accessed=2 * sum(x.size for x in operands), transcendentals=0)
    in_specs = [in_smem, in_smem, in_vmem if make else in_smem] + [anywhere] * len(operands)
    out_shape = [jax.ShapeDtypeStruct((size, block, lanes), jnp.bfloat16) for _, size in strips]
    scratch = [
        pltpu.VMEM((positions, spans + 1, block, lanes), jnp.bfloat16),
        pltpu.SemaphoreType.DMA((left_moves,)),
        pltpu.VMEM((groups, count, block, lanes), jnp.bfloat16),
        pltpu.SemaphoreType.DMA((panel_moves(strips),)),
    ]
    if make:
        out_shape.append(jax.ShapeDtypeStruct((groups, lanes), jnp.int32))
        scratch += [
            pltpu.SMEM((groups, lanes), jnp.int32),
            pltpu.VMEM((groups, ROWS, lanes), jnp.bfloat16),
            pltpu.SemaphoreType.DMA((groups,)),
            pltpu.SemaphoreType.DMA,
        ]
    out = pl.pallas_call(
        body,
        in_specs=in_specs,
        out_specs=[in_vmem] * len(out_shape),
        out_shape=out_shape,
        scratch_shapes=scratch,
        compiler_params=pltpu.CompilerParams(vmem_limit_bytes=60 * MIB),
        cost_estimate=cost,
    )(rows_at, groups_at, expected if make else table, *operands)
    return (out[:-1], out[-1]) if make else (out, table)


def second_product(table, rows_at, groups_at, slab, panels, strips, spans, scale, square, own):
    positions = SIDE * CORES
    groups = 2 * positions
    block, lanes = own.shape[-2:]
    left_moves = sum(len(ranges) for _, _, ranges in slab)
    members, flat_strips = {}, []
    for part, part_strips in enumerate(strips):
        inside = 0
        for first, size in part_strips:
            at = sum(size for _, size in flat_strips)
            members.update({first + m: (part, inside + m, at + m) for m in range(size)})
            flat_strips.append((first, size))
            inside += size
    starts = [sum(size for _, size in flat_strips[:i]) for i in range(len(flat_strips))]

    def body(table_ref, rows_ref, groups_ref, *refs):
        refs = list(refs)
        slab_refs = [refs.pop(0) for _ in slab]
        piece_refs = [[refs.pop(0) for _ in pieces] for pieces, _ in panels]
        square_refs = [refs.pop(0) for _ in square]
        own_ref, square_ref, flat_ref, left_ref, left_sem, right_ref, right_sem, done_ref = refs
        left_copies = slab_copies(slab_refs, slab, rows_ref, left_ref, left_sem)
        runs = panel_copies(piece_refs, panels, starts, flat_strips, 1, groups_ref, right_ref, right_sem)
        for copy in left_copies + runs[0][0]:
            copy.start()
        left_ref[:, spans] = jnp.zeros((positions, block, lanes), left_ref.dtype)
        join_columns(lambda m: square_refs[members[m][0]][members[m][1]], square_ref, spans, block)
        for copy in left_copies:
            copy.wait()
        for copies, _, _, _ in runs[1:]:
            for copy in copies:
                copy.start()

        def finish(member, at, sums):
            own_part = 1.5 * own_ref[member].astype(jnp.float32)
            done_ref[at] = (own_part - (0.5 * scale) * sums).astype(done_ref.dtype)

        run = block_sums(table_ref, left_ref, right_ref, spans, finish)
        for copies, first, at, size in runs:
            for copy in copies:
                copy.wait()
            run(first, at, size)
        join_columns(lambda m: done_ref[members[m][2]], flat_ref, spans, block)

    anywhere = pl.BlockSpec(memory_space=pl.ANY)
    in_vmem = pl.BlockSpec(memory_space=pltpu.VMEM)
    in_smem = pl.BlockSpec(memory_space=pltpu.SMEM)
    operands = [array for array, _, _ in slab] + [x for pieces, _ in panels for x, _, _ in pieces]
    flops = WEIGHT * spans * block * lanes * groups * block
    cost = pl.CostEstimate(flops=flops, bytes_accessed=2 * sum(x.size for x in operands), transcendentals=0)
    flat = jax.ShapeDtypeStruct((block, spans * lanes), jnp.bfloat16)
    return pl.pallas_call(
        body,
        in_specs=[in_smem] * 3 + [anywhere] * len(operands) + [in_vmem] * (len(square) + 1),
        out_specs=[in_vmem] * 2,
        out_shape=[flat] * 2,
        scratch_shapes=[
            pltpu.VMEM((positions, spans + 1, block, lanes), jnp.bfloat16),
            pltpu.SemaphoreType.DMA((left_moves,)),
            pltpu.VMEM((groups, spans, block, lanes), jnp.bfloat16),
            pltpu.SemaphoreType.DMA((panel_moves(flat_strips),)),
            pltpu.VMEM((spans, block, lanes), jnp.bfloat16),
        ],
        compiler_params=pltpu.CompilerParams(vmem_limit_bytes=60 * MIB),
        cost_estimate=cost,
    )(table, rows_at, groups_at, *operands, *square, own)


def per_device(values, pattern):
    block = values.shape[0]
    rows_here = values.shape[1] // block
    groups = lax.axis_size("col")
    spans = pattern.shape[0] // groups
    mine, group = lax.axis_index("row"), lax.axis_index("col")
    z, y = group // SIDE, group % SIDE
    column = pattern[:, 0]
    scale = 1.0 / math.sqrt(groups * block)

    split = (spans + 1) // 2
    halves = [(0, split), (split, spans - split)]
    own_links = lax.dynamic_slice_in_dim(column, mine * rows_here, rows_here, 0)
    own, *pieces = pair_columns(values, own_links, spans, halves)
    lines = []
    for axis, piece in enumerate(pieces):
        *three, (low, _, _), (high, _, _) = col_ring(piece, axis)
        lines.append([x for x, _, _ in three] + [jnp.concatenate([low, high], axis=0)])
    on_1 = sent_row(own, 1, 0)
    lines, on_1 = lax.optimization_barrier((lines, on_1))
    on_2 = sent_row(on_1, 1, 0)
    on_3 = sent_row(on_2, 1, 0)

    chip, core = mine // CORES, mine % CORES
    rows_at = [((chip + t) % SIDE) * CORES + (core + swap) % CORES for t in TURNS for swap in range(CORES)]
    groups_at = [((z + t) % SIDE) * SIDE + (y + u) % SIDE for t in TURNS for u in TURNS]
    rows_at = jnp.stack(rows_at).astype(jnp.int32)
    groups_at = jnp.stack(groups_at).astype(jnp.int32)
    member = jnp.arange(spans, dtype=jnp.int32)
    found = column.reshape(groups, spans, 1) == own_links[None, None, :]
    expected = jnp.sum(jnp.where(found, member[None, :, None], 0), axis=1)
    expected = expected + spans * jnp.arange(groups, dtype=jnp.int32)[:, None]
    expected = jnp.pad(expected, ((0, 0), (0, 2 * block - rows_here)), constant_values=-1)

    planes = [col_ring(jnp.concatenate(line, axis=0), 1 - axis) for axis, line in enumerate(lines)]
    nearest = [x for plane in planes for x, place, _ in plane if place in (1, 2)]
    chips, _ = lax.optimization_barrier(((own, on_1, on_2, on_3), nearest))
    first_slab = swapped_slab(chips)
    panels = [(plane, axis) for axis, plane in enumerate(planes)]
    squares, table = first_product(
        None, expected, rows_at, groups_at, first_slab, panels, halves, spans, scale
    )
    second_slab = halves_slab(*squares, halves)
    all_strips = [[strip] for strip in halves]
    where = (table, rows_at, groups_at)
    return tuple(second_product(*where, second_slab, panels, all_strips, spans, scale, squares, own))


def solution(mesh):
    in_specs = (P("col", "row"), P(None, "col"))
    out_specs = (P("col", "row"), P("col", "row"))
    return jax.shard_map(
        per_device, mesh=mesh, in_specs=in_specs, out_specs=out_specs, check_vma=False
    )
```

```python
import math

import jax
import jax.numpy as jnp
from jax import lax
from jax.experimental import pallas as pl
from jax.experimental.pallas import tpu as pltpu
from jax.sharding import PartitionSpec as P

TURNS = (0, -1, 1, 2)
CORES = 2
SIDE = 4
DIGIT = 32
CHUNK = 12
STEP = 6
WEIGHT = 48
ROWS = 16
MIB = 1024 * 1024


def pair_columns(values, links, spans, halves):
    block = values.shape[0]
    lanes = 2 * block

    def body(flat_ref, links_ref, whole_ref, *half_refs):
        for (start, size), ref in zip(halves, half_refs):
            for m in range(start, start + size):
                first = flat_ref[:, m * block : (m + 1) * block]
                second = flat_ref[:, (spans + m) * block : (spans + m + 1) * block]
                both = jnp.concatenate([first, second], axis=1)
                whole_ref[m] = both
                ref[m - start] = both
        row = lax.broadcasted_iota(jnp.int32, (block, lanes), 0)
        numbers = jnp.broadcast_to(links_ref[...], (block, lanes))
        digits = jnp.where(row == 0, numbers // DIGIT, numbers % DIGIT)
        half_refs[0][halves[0][1]] = digits.astype(jnp.float32).astype(values.dtype)

    sizes = [spans, halves[0][1] + 1, halves[1][1]]
    padded = jnp.pad(links, (0, lanes - links.shape[0])).reshape(1, lanes)
    return pl.pallas_call(
        body,
        out_shape=[jax.ShapeDtypeStruct((size, block, lanes), values.dtype) for size in sizes],
        compiler_params=pltpu.CompilerParams(vmem_limit_bytes=16 * MIB),
    )(values, padded)


def join_columns(pick, flat_ref, spans, block):
    for m in range(spans):
        both = pick(m)
        flat_ref[:, m * block : (m + 1) * block] = both[:, :block]
        flat_ref[:, (spans + m) * block : (spans + m + 1) * block] = both[:, block:]


def sent_row(array, turn, swap):
    chips = lax.axis_size("row") // CORES
    order = [
        (x * CORES + c, ((x - turn) % chips) * CORES + (c + swap) % CORES)
        for x in range(chips)
        for c in range(CORES)
    ]
    return lax.ppermute(array, "row", order)


def sent_col(array, turn, axis):
    step = (turn, 0) if axis == 0 else (0, turn)
    order = [
        (z * SIDE + y, ((z - step[0]) % SIDE) * SIDE + (y - step[1]) % SIDE)
        for z in range(SIDE)
        for y in range(SIDE)
    ]
    return lax.ppermute(array, "col", order)


def ring(array, sent, nearest=None):
    size = array.shape[0]
    half = (size + 1) // 2
    behind, ahead = nearest or (sent(array, -1), sent(array, 1))
    low = sent(lax.slice_in_dim(ahead, 0, half, axis=0), 1)
    high = sent(lax.slice_in_dim(behind, half, size, axis=0), -1)
    return [(array, 0, 0), (behind, 1, 0), (ahead, 2, 0), (low, 3, 0), (high, 3, half)]


def col_ring(array, axis):
    return ring(array, lambda x, turn: sent_col(x, turn, axis))


def row_slab(array, strips):
    behind, ahead, swapped = sent_row(array, -1, 0), sent_row(array, 1, 0), sent_row(array, 0, 1)
    nearest = lax.optimization_barrier((behind, ahead, swapped))
    near = ring(array, lambda x, turn: sent_row(x, turn, 0), nearest[:2])
    slab = []
    for piece, turn, begin in near:
        end, at, ranges = begin + piece.shape[0], 0, []
        for start, size in strips:
            low, high = max(at, begin), min(at + size, end)
            if low < high:
                ranges.append((low - begin, start + low - at, high - low))
            at += size
        slab.append((piece, turn * CORES, ranges))
        other = nearest[2] if turn == 0 else sent_row(piece, 0, 1)
        slab.append((other, turn * CORES + 1, ranges))
    return slab


def halves_slab(low, high, strips):
    ahead_low, behind_high = sent_row(low, 1, 0), sent_row(high, -1, 0)
    ahead_high, behind_low = sent_row(high, 1, 0), sent_row(low, -1, 0)
    far = (sent_row(ahead_low, 1, 0), sent_row(behind_high, -1, 0))
    slab = []
    chips = [(low, high), (behind_low, behind_high), (ahead_low, ahead_high), far]
    for turn, pair in enumerate(chips):
        for x, (start, size) in zip(pair, strips):
            slab.append((x, turn * CORES, [(0, start, size)]))
            slab.append((sent_row(x, 0, 1), turn * CORES + 1, [(0, start, size)]))
    return slab


def swapped_slab(chips):
    size = chips[0].shape[0]
    swapped = sent_row(jnp.concatenate(chips, axis=0), 0, 1)
    slab = []
    for step, x in enumerate(chips):
        place = CORES * TURNS.index((step + 1) % SIDE - 1)
        slab += [(x, place, [(0, 0, size)]), (swapped, place + 1, [(step * size, 0, size)])]
    return slab


def slab_copies(refs, slab, rows_ref, left_ref, sems):
    copies = []
    for ref, (_, place, ranges) in zip(refs, slab):
        for offset, start, size in ranges:
            source = ref.at[pl.ds(offset, size)]
            target = left_ref.at[rows_ref[place], pl.ds(start, size)]
            copies.append(pltpu.make_async_copy(source, target, sems.at[len(copies)]))
    return copies


def pieces_of(size, strip):
    edges = list(range(STEP if strip == 0 else 0, size, CHUNK))
    edges = sorted({0, *edges, size})
    return [(a, b - a) for a, b in zip(edges[:-1], edges[1:])]


def panel_copies(refs, panels, starts, strips, more, groups_ref, right_ref, sems):
    runs, used = [], 0
    for strip, (refs_here, (pieces, axis), at, (member, size)) in enumerate(zip(refs, panels, starts, strips)):
        stride = size + (more if strip == 0 else 0)
        for a, some in pieces_of(size, strip):
            copies = []
            for ref, (array, second, begin) in zip(refs_here, pieces):
                for first in range(SIDE):
                    offset = first * stride - begin
                    if 0 <= offset < array.shape[0]:
                        slot = first * SIDE + second if axis == 0 else second * SIDE + first
                        source = ref.at[pl.ds(offset + a, some)]
                        target = right_ref.at[groups_ref[slot], pl.ds(at + a, some)]
                        copies.append(pltpu.make_async_copy(source, target, sems.at[used]))
                        used += 1
            runs.append((copies, member + a, at + a, some))
    return runs


def panel_moves(strips):
    return SIDE * SIDE * sum(len(pieces_of(size, i)) for i, (_, size) in enumerate(strips))


def block_sums(table_ref, left_ref, right_ref, spans, finish):
    positions = left_ref.shape[0]
    groups, _, block, lanes = right_ref.shape
    low = lax.broadcasted_iota(jnp.int32, (block, lanes), 1) < block

    def strip_of(member, e):
        row = e * spans + member
        return jnp.concatenate(
            [
                jnp.where(low, left_ref[j, table_ref[2 * j, row]], left_ref[j, table_ref[2 * j + 1, row]])
                for j in range(positions)
            ],
            axis=1,
        )

    def members(first, at, number):
        rows = [strip_of(first + u, e) for u in range(number) for e in range(2)]
        columns = [right_ref[:, at + u].reshape(groups * block, lanes) for u in range(number)]
        sums = jnp.dot(
            jnp.concatenate(rows, axis=0),
            jnp.concatenate(columns, axis=1),
            preferred_element_type=jnp.float32,
        )
        for u in range(number):
            across = slice(u * lanes, (u + 1) * lanes)
            top = 2 * u * block
            upper, lower = sums[top : top + block, across], sums[top + block : top + 2 * block, across]
            finish(first + u, at + u, jnp.where(low, upper, lower))

    def run(first, at, size):
        def step(t, carry):
            for u in range(0, STEP, 2):
                members(first + STEP * t + u, at + STEP * t + u, 2)
            return carry

        lax.fori_loop(0, size // STEP, step, 0)
        for u in range(size // STEP * STEP, size - 1, 2):
            members(first + u, at + u, 2)
        if size % 2:
            members(first + size - 1, at + size - 1, 1)

    return run


def first_product(table, expected, rows_at, groups_at, slab, panels, strips, spans, scale):
    positions = SIDE * CORES
    groups = 2 * positions
    block, lanes = slab[0][0].shape[-2:]
    starts = [sum(size for _, size in strips[:i]) for i in range(len(strips))]
    count = sum(size for _, size in strips)
    make = table is None
    left_moves = sum(len(ranges) for _, _, ranges in slab)

    def body(rows_ref, groups_ref, *refs):
        refs = list(refs)
        if make:
            expected_ref = refs.pop(0)
        else:
            table_ref = refs.pop(0)
        slab_refs = [refs.pop(0) for _ in slab]
        piece_refs = [[refs.pop(0) for _ in pieces] for pieces, _ in panels]
        out_refs = [refs.pop(0) for _ in strips]
        done_refs, done_sem = [refs.pop() for _ in strips][::-1], refs.pop()
        out_copies = [
            pltpu.make_async_copy(ref, out, done_sem.at[i])
            for i, (ref, out) in enumerate(zip(done_refs, out_refs))
        ]
        if make:
            table_out, left_ref, left_sem, right_ref, right_sem, table_ref, extra_ref, extra_sem, table_sem = refs
        else:
            left_ref, left_sem, right_ref, right_sem = refs

        runs = panel_copies(piece_refs, panels, starts, strips, int(make), groups_ref, right_ref, right_sem)
        extra_copies = []
        if make:
            (pieces, axis), size = panels[0], strips[0][1]
            for ref, (array, second, begin) in zip(piece_refs[0], pieces):
                for first in range(SIDE):
                    offset = first * (size + 1) - begin
                    if 0 <= offset < array.shape[0]:
                        slot = first * SIDE + second if axis == 0 else second * SIDE + first
                        source = ref.at[offset + size, pl.ds(0, ROWS)]
                        target = extra_ref.at[groups_ref[slot]]
                        sem = extra_sem.at[len(extra_copies)]
                        extra_copies.append(pltpu.make_async_copy(source, target, sem))
        left_copies = slab_copies(slab_refs, slab, rows_ref, left_ref, left_sem)
        for copy in extra_copies + left_copies + runs[0][0]:
            copy.start()
        left_ref[:, spans] = jnp.zeros((positions, block, lanes), left_ref.dtype)
        if make:
            for copy in extra_copies:
                copy.wait()
            row = lax.broadcasted_iota(jnp.int32, (groups, ROWS, lanes), 1)
            weights = jnp.where(row == 0, DIGIT, jnp.where(row == 1, 1, 0)).astype(jnp.float32)
            links = jnp.sum(extra_ref[...].astype(jnp.float32) * weights, axis=1).astype(jnp.int32)
            wanted = expected_ref[...]
            first_of = spans * lax.broadcasted_iota(jnp.int32, (groups, lanes), 0)
            table_out[...] = jnp.where(links == wanted, wanted - first_of, spans)
            copy = pltpu.make_async_copy(table_out, table_ref, table_sem)
            copy.start()
            copy.wait()
        for copy in left_copies:
            copy.wait()
        for copies, _, _, _ in runs[1:]:
            for copy in copies:
                copy.start()

        for copies, first, at, size in runs:
            for copy in copies:
                copy.wait()
            strip = max(i for i, start in enumerate(starts) if start <= at)

            def finish(member, at, sums, done_ref=done_refs[strip], start=starts[strip]):
                done_ref[at - start] = (sums * scale).astype(done_ref.dtype)

            block_sums(table_ref, left_ref, right_ref, spans, finish)(first, at, size)
            if at + size == starts[strip] + strips[strip][1]:
                out_copies[strip].start()
        for copy in out_copies:
            copy.wait()

    anywhere = pl.BlockSpec(memory_space=pl.ANY)
    in_vmem = pl.BlockSpec(memory_space=pltpu.VMEM)
    in_smem = pl.BlockSpec(memory_space=pltpu.SMEM)
    operands = [array for array, _, _ in slab] + [x for pieces, _ in panels for x, _, _ in pieces]
    flops = WEIGHT * count * block * lanes * groups * block
    cost = pl.CostEstimate(flops=flops, bytes_accessed=2 * sum(x.size for x in operands), transcendentals=0)
    in_specs = [in_smem, in_smem, in_vmem if make else in_smem] + [anywhere] * len(operands)
    out_shape = [jax.ShapeDtypeStruct((size, block, lanes), jnp.bfloat16) for _, size in strips]
    scratch = [
        pltpu.VMEM((positions, spans + 1, block, lanes), jnp.bfloat16),
        pltpu.SemaphoreType.DMA((left_moves,)),
        pltpu.VMEM((groups, count, block, lanes), jnp.bfloat16),
        pltpu.SemaphoreType.DMA((panel_moves(strips),)),
    ]
    if make:
        out_shape.append(jax.ShapeDtypeStruct((groups, lanes), jnp.int32))
        scratch += [
            pltpu.SMEM((groups, lanes), jnp.int32),
            pltpu.VMEM((groups, ROWS, lanes), jnp.bfloat16),
            pltpu.SemaphoreType.DMA((groups,)),
            pltpu.SemaphoreType.DMA,
        ]
    scratch.append(pltpu.SemaphoreType.DMA((len(strips),)))
    scratch += [pltpu.VMEM((size, block, lanes), jnp.bfloat16) for _, size in strips]
    out = pl.pallas_call(
        body,
        in_specs=in_specs,
        out_specs=[anywhere] * len(strips) + [in_vmem] * int(make),
        out_shape=out_shape,
        scratch_shapes=scratch,
        compiler_params=pltpu.CompilerParams(vmem_limit_bytes=60 * MIB),
        cost_estimate=cost,
    )(rows_at, groups_at, expected if make else table, *operands)
    return (out[:-1], out[-1]) if make else (out, table)


def second_product(table, rows_at, groups_at, slab, panels, strips, spans, scale, square, own):
    positions = SIDE * CORES
    groups = 2 * positions
    block, lanes = own.shape[-2:]
    left_moves = sum(len(ranges) for _, _, ranges in slab)
    members, flat_strips = {}, []
    for part, part_strips in enumerate(strips):
        inside = 0
        for first, size in part_strips:
            at = sum(size for _, size in flat_strips)
            members.update({first + m: (part, inside + m, at + m) for m in range(size)})
            flat_strips.append((first, size))
            inside += size
    starts = [sum(size for _, size in flat_strips[:i]) for i in range(len(flat_strips))]

    def body(table_ref, rows_ref, groups_ref, *refs):
        refs = list(refs)
        slab_refs = [refs.pop(0) for _ in slab]
        piece_refs = [[refs.pop(0) for _ in pieces] for pieces, _ in panels]
        square_refs = [refs.pop(0) for _ in square]
        own_ref, square_out, flat_ref, left_ref, left_sem, right_ref, right_sem, done_ref = refs[:8]
        square_ref, square_sem = refs[8:]
        square_copy = pltpu.make_async_copy(square_ref, square_out, square_sem)
        left_copies = slab_copies(slab_refs, slab, rows_ref, left_ref, left_sem)
        runs = panel_copies(piece_refs, panels, starts, flat_strips, 1, groups_ref, right_ref, right_sem)
        for copy in left_copies + runs[0][0]:
            copy.start()
        left_ref[:, spans] = jnp.zeros((positions, block, lanes), left_ref.dtype)
        join_columns(lambda m: square_refs[members[m][0]][members[m][1]], square_ref, spans, block)
        square_copy.start()
        for copy in left_copies:
            copy.wait()
        for copies, _, _, _ in runs[1:]:
            for copy in copies:
                copy.start()

        def finish(member, at, sums):
            own_part = 1.5 * own_ref[member].astype(jnp.float32)
            done_ref[at] = (own_part - (0.5 * scale) * sums).astype(done_ref.dtype)

        run = block_sums(table_ref, left_ref, right_ref, spans, finish)
        for copies, first, at, size in runs:
            for copy in copies:
                copy.wait()
            run(first, at, size)
        join_columns(lambda m: done_ref[members[m][2]], flat_ref, spans, block)
        square_copy.wait()

    anywhere = pl.BlockSpec(memory_space=pl.ANY)
    in_vmem = pl.BlockSpec(memory_space=pltpu.VMEM)
    in_smem = pl.BlockSpec(memory_space=pltpu.SMEM)
    operands = [array for array, _, _ in slab] + [x for pieces, _ in panels for x, _, _ in pieces]
    flops = WEIGHT * spans * block * lanes * groups * block
    cost = pl.CostEstimate(flops=flops, bytes_accessed=2 * sum(x.size for x in operands), transcendentals=0)
    flat = jax.ShapeDtypeStruct((block, spans * lanes), jnp.bfloat16)
    return pl.pallas_call(
        body,
        in_specs=[in_smem] * 3 + [anywhere] * len(operands) + [in_vmem] * (len(square) + 1),
        out_specs=[anywhere, in_vmem],
        out_shape=[flat] * 2,
        scratch_shapes=[
            pltpu.VMEM((positions, spans + 1, block, lanes), jnp.bfloat16),
            pltpu.SemaphoreType.DMA((left_moves,)),
            pltpu.VMEM((groups, spans, block, lanes), jnp.bfloat16),
            pltpu.SemaphoreType.DMA((panel_moves(flat_strips),)),
            pltpu.VMEM((spans, block, lanes), jnp.bfloat16),
            pltpu.VMEM((block, spans * lanes), jnp.bfloat16),
            pltpu.SemaphoreType.DMA,
        ],
        compiler_params=pltpu.CompilerParams(vmem_limit_bytes=60 * MIB),
        cost_estimate=cost,
    )(table, rows_at, groups_at, *operands, *square, own)


def per_device(values, pattern):
    block = values.shape[0]
    rows_here = values.shape[1] // block
    groups = lax.axis_size("col")
    spans = pattern.shape[0] // groups
    mine, group = lax.axis_index("row"), lax.axis_index("col")
    z, y = group // SIDE, group % SIDE
    column = pattern[:, 0]
    scale = 1.0 / math.sqrt(groups * block)

    split = (spans + 1) // 2 + 1
    halves = [(0, split), (split, spans - split)]
    own_links = lax.dynamic_slice_in_dim(column, mine * rows_here, rows_here, 0)
    own, *pieces = pair_columns(values, own_links, spans, halves)
    lines = []
    for axis, piece in enumerate(pieces):
        *three, (low, _, _), (high, _, _) = col_ring(piece, axis)
        lines.append([x for x, _, _ in three] + [jnp.concatenate([low, high], axis=0)])
    on_1 = sent_row(own, 1, 0)
    lines, on_1 = lax.optimization_barrier((lines, on_1))
    on_2 = sent_row(on_1, 1, 0)
    on_3 = sent_row(on_2, 1, 0)

    chip, core = mine // CORES, mine % CORES
    rows_at = [((chip + t) % SIDE) * CORES + (core + swap) % CORES for t in TURNS for swap in range(CORES)]
    groups_at = [((z + t) % SIDE) * SIDE + (y + u) % SIDE for t in TURNS for u in TURNS]
    rows_at = jnp.stack(rows_at).astype(jnp.int32)
    groups_at = jnp.stack(groups_at).astype(jnp.int32)
    member = jnp.arange(spans, dtype=jnp.int32)
    found = column.reshape(groups, spans, 1) == own_links[None, None, :]
    expected = jnp.sum(jnp.where(found, member[None, :, None], 0), axis=1)
    expected = expected + spans * jnp.arange(groups, dtype=jnp.int32)[:, None]
    expected = jnp.pad(expected, ((0, 0), (0, 2 * block - rows_here)), constant_values=-1)

    planes = [col_ring(jnp.concatenate(line, axis=0), 1 - axis) for axis, line in enumerate(lines)]
    nearest = [x for plane in planes for x, place, _ in plane if place in (1, 2)]
    chips, _ = lax.optimization_barrier(((own, on_1, on_2, on_3), nearest))
    first_slab = swapped_slab(chips)
    panels = [(plane, axis) for axis, plane in enumerate(planes)]
    squares, table = first_product(
        None, expected, rows_at, groups_at, first_slab, panels, halves, spans, scale
    )
    second_slab = halves_slab(*squares, halves)
    all_strips = [[strip] for strip in halves]
    where = (table, rows_at, groups_at)
    return tuple(second_product(*where, second_slab, panels, all_strips, spans, scale, squares, own))


def solution(mesh):
    in_specs = (P("col", "row"), P(None, "col"))
    out_specs = (P("col", "row"), P("col", "row"))
    return jax.shard_map(
        per_device, mesh=mesh, in_specs=in_specs, out_specs=out_specs, check_vma=False
    )
```

```python
import math

import jax
import jax.numpy as jnp
from jax import lax
from jax.experimental import pallas as pl
from jax.experimental.pallas import tpu as pltpu
from jax.sharding import PartitionSpec as P

TURNS = (0, -1, 1, 2)
CORES = 2
SIDE = 4
DIGIT = 32
CHUNK = 12
STEP = 6
WEIGHT = 48
ROWS = 16
MIB = 1024 * 1024


def pair_columns(values, links, spans, halves):
    block = values.shape[0]
    lanes = 2 * block

    def body(flat_ref, links_ref, whole_ref, *half_refs):
        for (start, size), ref in zip(halves, half_refs):
            for m in range(start, start + size):
                first = flat_ref[:, m * block : (m + 1) * block]
                second = flat_ref[:, (spans + m) * block : (spans + m + 1) * block]
                both = jnp.concatenate([first, second], axis=1)
                whole_ref[m] = both
                ref[m - start] = both
        row = lax.broadcasted_iota(jnp.int32, (block, lanes), 0)
        numbers = jnp.broadcast_to(links_ref[...], (block, lanes))
        digits = jnp.where(row == 0, numbers // DIGIT, numbers % DIGIT)
        half_refs[0][halves[0][1]] = digits.astype(jnp.float32).astype(values.dtype)

    sizes = [spans, halves[0][1] + 1, halves[1][1]]
    padded = jnp.pad(links, (0, lanes - links.shape[0])).reshape(1, lanes)
    return pl.pallas_call(
        body,
        out_shape=[jax.ShapeDtypeStruct((size, block, lanes), values.dtype) for size in sizes],
        compiler_params=pltpu.CompilerParams(vmem_limit_bytes=16 * MIB),
    )(values, padded)


def join_columns(pick, flat_ref, spans, block):
    for m in range(spans):
        both = pick(m)
        flat_ref[:, m * block : (m + 1) * block] = both[:, :block]
        flat_ref[:, (spans + m) * block : (spans + m + 1) * block] = both[:, block:]


def sent_row(array, turn, swap):
    chips = lax.axis_size("row") // CORES
    order = [
        (x * CORES + c, ((x - turn) % chips) * CORES + (c + swap) % CORES)
        for x in range(chips)
        for c in range(CORES)
    ]
    return lax.ppermute(array, "row", order)


def sent_col(array, turn, axis):
    step = (turn, 0) if axis == 0 else (0, turn)
    order = [
        (z * SIDE + y, ((z - step[0]) % SIDE) * SIDE + (y - step[1]) % SIDE)
        for z in range(SIDE)
        for y in range(SIDE)
    ]
    return lax.ppermute(array, "col", order)


def ring(array, sent, nearest=None, marks=None):
    size = array.shape[0]
    half = (size + 1) // 2
    behind, ahead = nearest or (sent(array, -1), sent(array, 1))
    low = lax.slice_in_dim(ahead, 0, half, axis=0)
    high = lax.slice_in_dim(behind, half, size, axis=0)
    if marks is not None:
        marks += [low, high]
    low, high = sent(low, 1), sent(high, -1)
    return [(array, 0, 0), (behind, 1, 0), (ahead, 2, 0), (low, 3, 0), (high, 3, half)]


def col_ring(array, axis, marks=None):
    return ring(array, lambda x, turn: sent_col(x, turn, axis), marks=marks)


def row_slab(array, strips):
    behind, ahead, swapped = sent_row(array, -1, 0), sent_row(array, 1, 0), sent_row(array, 0, 1)
    nearest = lax.optimization_barrier((behind, ahead, swapped))
    near = ring(array, lambda x, turn: sent_row(x, turn, 0), nearest[:2])
    slab = []
    for piece, turn, begin in near:
        end, at, ranges = begin + piece.shape[0], 0, []
        for start, size in strips:
            low, high = max(at, begin), min(at + size, end)
            if low < high:
                ranges.append((low - begin, start + low - at, high - low))
            at += size
        slab.append((piece, turn * CORES, ranges))
        other = nearest[2] if turn == 0 else sent_row(piece, 0, 1)
        slab.append((other, turn * CORES + 1, ranges))
    return slab


def halves_slab(low, high, strips):
    ahead_low, behind_high = sent_row(low, 1, 0), sent_row(high, -1, 0)
    ahead_high, behind_low = sent_row(high, 1, 0), sent_row(low, -1, 0)
    far = (sent_row(ahead_low, 1, 0), sent_row(behind_high, -1, 0))
    slab = []
    chips = [(low, high), (behind_low, behind_high), (ahead_low, ahead_high), far]
    for turn, pair in enumerate(chips):
        for x, (start, size) in zip(pair, strips):
            slab.append((x, turn * CORES, [(0, start, size)]))
            slab.append((sent_row(x, 0, 1), turn * CORES + 1, [(0, start, size)]))
    return slab


def swapped_slab(chips):
    size = chips[0].shape[0]
    swapped = sent_row(jnp.concatenate(chips, axis=0), 0, 1)
    slab = []
    for step, x in enumerate(chips):
        place = CORES * TURNS.index((step + 1) % SIDE - 1)
        slab += [(x, place, [(0, 0, size)]), (swapped, place + 1, [(step * size, 0, size)])]
    return slab


def slab_copies(refs, slab, rows_ref, left_ref, sems):
    copies = []
    for ref, (_, place, ranges) in zip(refs, slab):
        for offset, start, size in ranges:
            source = ref.at[pl.ds(offset, size)]
            target = left_ref.at[rows_ref[place], pl.ds(start, size)]
            copies.append(pltpu.make_async_copy(source, target, sems.at[len(copies)]))
    return copies


def pieces_of(size, strip):
    edges = list(range(STEP if strip == 0 else 0, size, CHUNK))
    edges = sorted({0, *edges, size})
    return [(a, b - a) for a, b in zip(edges[:-1], edges[1:])]


def panel_copies(refs, panels, starts, strips, more, groups_ref, right_ref, sems):
    runs, used = [], 0
    for strip, (refs_here, (pieces, axis), at, (member, size)) in enumerate(zip(refs, panels, starts, strips)):
        stride = size + (more if strip == 0 else 0)
        for a, some in pieces_of(size, strip):
            copies = []
            for ref, (array, second, begin) in zip(refs_here, pieces):
                for first in range(SIDE):
                    offset = first * stride - begin
                    if 0 <= offset < array.shape[0]:
                        slot = first * SIDE + second if axis == 0 else second * SIDE + first
                        source = ref.at[pl.ds(offset + a, some)]
                        target = right_ref.at[groups_ref[slot], pl.ds(at + a, some)]
                        copies.append(pltpu.make_async_copy(source, target, sems.at[used]))
                        used += 1
            runs.append((copies, member + a, at + a, some))
    return runs


def panel_moves(strips):
    return SIDE * SIDE * sum(len(pieces_of(size, i)) for i, (_, size) in enumerate(strips))


def block_sums(table_ref, left_ref, right_ref, spans, finish):
    positions = left_ref.shape[0]
    groups, _, block, lanes = right_ref.shape
    low = lax.broadcasted_iota(jnp.int32, (block, lanes), 1) < block

    def strip_of(member, e):
        row = e * spans + member
        return jnp.concatenate(
            [
                jnp.where(low, left_ref[j, table_ref[2 * j, row]], left_ref[j, table_ref[2 * j + 1, row]])
                for j in range(positions)
            ],
            axis=1,
        )

    def members(first, at, number):
        rows = [strip_of(first + u, e) for u in range(number) for e in range(2)]
        columns = [right_ref[:, at + u].reshape(groups * block, lanes) for u in range(number)]
        sums = jnp.dot(
            jnp.concatenate(rows, axis=0),
            jnp.concatenate(columns, axis=1),
            preferred_element_type=jnp.float32,
        )
        for u in range(number):
            across = slice(u * lanes, (u + 1) * lanes)
            top = 2 * u * block
            upper, lower = sums[top : top + block, across], sums[top + block : top + 2 * block, across]
            finish(first + u, at + u, jnp.where(low, upper, lower))

    def run(first, at, size):
        def step(t, carry):
            for u in range(0, STEP, 2):
                members(first + STEP * t + u, at + STEP * t + u, 2)
            return carry

        lax.fori_loop(0, size // STEP, step, 0)
        for u in range(size // STEP * STEP, size - 1, 2):
            members(first + u, at + u, 2)
        if size % 2:
            members(first + size - 1, at + size - 1, 1)

    return run


def first_product(table, expected, rows_at, groups_at, slab, panels, strips, spans, scale):
    positions = SIDE * CORES
    groups = 2 * positions
    block, lanes = slab[0][0].shape[-2:]
    starts = [sum(size for _, size in strips[:i]) for i in range(len(strips))]
    count = sum(size for _, size in strips)
    make = table is None
    left_moves = sum(len(ranges) for _, _, ranges in slab)

    def body(rows_ref, groups_ref, *refs):
        refs = list(refs)
        if make:
            expected_ref = refs.pop(0)
        else:
            table_ref = refs.pop(0)
        slab_refs = [refs.pop(0) for _ in slab]
        piece_refs = [[refs.pop(0) for _ in pieces] for pieces, _ in panels]
        done_refs = [refs.pop(0) for _ in strips]
        if make:
            table_out, left_ref, left_sem, right_ref, right_sem, table_ref, extra_ref, extra_sem, table_sem = refs
        else:
            left_ref, left_sem, right_ref, right_sem = refs

        runs = panel_copies(piece_refs, panels, starts, strips, int(make), groups_ref, right_ref, right_sem)
        extra_copies = []
        if make:
            (pieces, axis), size = panels[0], strips[0][1]
            for ref, (array, second, begin) in zip(piece_refs[0], pieces):
                for first in range(SIDE):
                    offset = first * (size + 1) - begin
                    if 0 <= offset < array.shape[0]:
                        slot = first * SIDE + second if axis == 0 else second * SIDE + first
                        source = ref.at[offset + size, pl.ds(0, ROWS)]
                        target = extra_ref.at[groups_ref[slot]]
                        sem = extra_sem.at[len(extra_copies)]
                        extra_copies.append(pltpu.make_async_copy(source, target, sem))
        left_copies = slab_copies(slab_refs, slab, rows_ref, left_ref, left_sem)
        for copy in extra_copies + left_copies + runs[0][0]:
            copy.start()
        left_ref[:, spans] = jnp.zeros((positions, block, lanes), left_ref.dtype)
        if make:
            for copy in extra_copies:
                copy.wait()
            row = lax.broadcasted_iota(jnp.int32, (groups, ROWS, lanes), 1)
            weights = jnp.where(row == 0, DIGIT, jnp.where(row == 1, 1, 0)).astype(jnp.float32)
            links = jnp.sum(extra_ref[...].astype(jnp.float32) * weights, axis=1).astype(jnp.int32)
            wanted = expected_ref[...]
            first_of = spans * lax.broadcasted_iota(jnp.int32, (groups, lanes), 0)
            table_out[...] = jnp.where(links == wanted, wanted - first_of, spans)
            copy = pltpu.make_async_copy(table_out, table_ref, table_sem)
            copy.start()
            copy.wait()
        for copy in left_copies:
            copy.wait()
        for copies, _, _, _ in runs[1:]:
            for copy in copies:
                copy.start()

        for copies, first, at, size in runs:
            for copy in copies:
                copy.wait()
            strip = max(i for i, start in enumerate(starts) if start <= at)

            def finish(member, at, sums, done_ref=done_refs[strip], start=starts[strip]):
                done_ref[at - start] = (sums * scale).astype(done_ref.dtype)

            block_sums(table_ref, left_ref, right_ref, spans, finish)(first, at, size)

    anywhere = pl.BlockSpec(memory_space=pl.ANY)
    in_vmem = pl.BlockSpec(memory_space=pltpu.VMEM)
    in_smem = pl.BlockSpec(memory_space=pltpu.SMEM)
    operands = [array for array, _, _ in slab] + [x for pieces, _ in panels for x, _, _ in pieces]
    flops = WEIGHT * count * block * lanes * groups * block
    cost = pl.CostEstimate(flops=flops, bytes_accessed=2 * sum(x.size for x in operands), transcendentals=0)
    in_specs = [in_smem, in_smem, in_vmem if make else in_smem] + [anywhere] * len(operands)
    out_shape = [jax.ShapeDtypeStruct((size, block, lanes), jnp.bfloat16) for _, size in strips]
    scratch = [
        pltpu.VMEM((positions, spans + 1, block, lanes), jnp.bfloat16),
        pltpu.SemaphoreType.DMA((left_moves,)),
        pltpu.VMEM((groups, count, block, lanes), jnp.bfloat16),
        pltpu.SemaphoreType.DMA((panel_moves(strips),)),
    ]
    if make:
        out_shape.append(jax.ShapeDtypeStruct((groups, lanes), jnp.int32))
        scratch += [
            pltpu.SMEM((groups, lanes), jnp.int32),
            pltpu.VMEM((groups, ROWS, lanes), jnp.bfloat16),
            pltpu.SemaphoreType.DMA((groups,)),
            pltpu.SemaphoreType.DMA,
        ]
    out = pl.pallas_call(
        body,
        in_specs=in_specs,
        out_specs=[in_vmem] * len(out_shape),
        out_shape=out_shape,
        scratch_shapes=scratch,
        compiler_params=pltpu.CompilerParams(vmem_limit_bytes=60 * MIB),
        cost_estimate=cost,
    )(rows_at, groups_at, expected if make else table, *operands)
    return (out[:-1], out[-1]) if make else (out, table)


def second_product(table, rows_at, groups_at, slab, panels, strips, spans, scale, square, own):
    positions = SIDE * CORES
    groups = 2 * positions
    block, lanes = own.shape[-2:]
    left_moves = sum(len(ranges) for _, _, ranges in slab)
    members, flat_strips = {}, []
    for part, part_strips in enumerate(strips):
        inside = 0
        for first, size in part_strips:
            at = sum(size for _, size in flat_strips)
            members.update({first + m: (part, inside + m, at + m) for m in range(size)})
            flat_strips.append((first, size))
            inside += size
    starts = [sum(size for _, size in flat_strips[:i]) for i in range(len(flat_strips))]

    def body(table_ref, rows_ref, groups_ref, *refs):
        refs = list(refs)
        slab_refs = [refs.pop(0) for _ in slab]
        piece_refs = [[refs.pop(0) for _ in pieces] for pieces, _ in panels]
        square_refs = [refs.pop(0) for _ in square]
        own_ref, square_ref, flat_ref, left_ref, left_sem, right_ref, right_sem, done_ref = refs
        left_copies = slab_copies(slab_refs, slab, rows_ref, left_ref, left_sem)
        runs = panel_copies(piece_refs, panels, starts, flat_strips, 1, groups_ref, right_ref, right_sem)
        for copy in left_copies + runs[0][0]:
            copy.start()
        left_ref[:, spans] = jnp.zeros((positions, block, lanes), left_ref.dtype)
        join_columns(lambda m: square_refs[members[m][0]][members[m][1]], square_ref, spans, block)
        for copy in left_copies:
            copy.wait()
        for copies, _, _, _ in runs[1:]:
            for copy in copies:
                copy.start()

        def finish(member, at, sums):
            own_part = 1.5 * own_ref[member].astype(jnp.float32)
            done_ref[at] = (own_part - (0.5 * scale) * sums).astype(done_ref.dtype)

        run = block_sums(table_ref, left_ref, right_ref, spans, finish)
        for copies, first, at, size in runs:
            for copy in copies:
                copy.wait()
            run(first, at, size)
        join_columns(lambda m: done_ref[members[m][2]], flat_ref, spans, block)

    anywhere = pl.BlockSpec(memory_space=pl.ANY)
    in_vmem = pl.BlockSpec(memory_space=pltpu.VMEM)
    in_smem = pl.BlockSpec(memory_space=pltpu.SMEM)
    operands = [array for array, _, _ in slab] + [x for pieces, _ in panels for x, _, _ in pieces]
    flops = WEIGHT * spans * block * lanes * groups * block
    cost = pl.CostEstimate(flops=flops, bytes_accessed=2 * sum(x.size for x in operands), transcendentals=0)
    flat = jax.ShapeDtypeStruct((block, spans * lanes), jnp.bfloat16)
    return pl.pallas_call(
        body,
        in_specs=[in_smem] * 3 + [anywhere] * len(operands) + [in_vmem] * (len(square) + 1),
        out_specs=[in_vmem] * 2,
        out_shape=[flat] * 2,
        scratch_shapes=[
            pltpu.VMEM((positions, spans + 1, block, lanes), jnp.bfloat16),
            pltpu.SemaphoreType.DMA((left_moves,)),
            pltpu.VMEM((groups, spans, block, lanes), jnp.bfloat16),
            pltpu.SemaphoreType.DMA((panel_moves(flat_strips),)),
            pltpu.VMEM((spans, block, lanes), jnp.bfloat16),
        ],
        compiler_params=pltpu.CompilerParams(vmem_limit_bytes=60 * MIB),
        cost_estimate=cost,
    )(table, rows_at, groups_at, *operands, *square, own)


def per_device(values, pattern):
    block = values.shape[0]
    rows_here = values.shape[1] // block
    groups = lax.axis_size("col")
    spans = pattern.shape[0] // groups
    mine, group = lax.axis_index("row"), lax.axis_index("col")
    z, y = group // SIDE, group % SIDE
    column = pattern[:, 0]
    scale = 1.0 / math.sqrt(groups * block)

    split = (spans + 1) // 2
    halves = [(0, split), (split, spans - split)]
    own_links = lax.dynamic_slice_in_dim(column, mine * rows_here, rows_here, 0)
    own, *pieces = pair_columns(values, own_links, spans, halves)
    lines = []
    for axis, piece in enumerate(pieces):
        *three, (low, _, _), (high, _, _) = col_ring(piece, axis)
        lines.append([x for x, _, _ in three] + [jnp.concatenate([low, high], axis=0)])
    on_1 = sent_row(own, 1, 0)
    lines, on_1 = lax.optimization_barrier((lines, on_1))
    on_2 = sent_row(on_1, 1, 0)
    on_3 = sent_row(on_2, 1, 0)

    chip, core = mine // CORES, mine % CORES
    rows_at = [((chip + t) % SIDE) * CORES + (core + swap) % CORES for t in TURNS for swap in range(CORES)]
    groups_at = [((z + t) % SIDE) * SIDE + (y + u) % SIDE for t in TURNS for u in TURNS]
    rows_at = jnp.stack(rows_at).astype(jnp.int32)
    groups_at = jnp.stack(groups_at).astype(jnp.int32)
    member = jnp.arange(spans, dtype=jnp.int32)
    found = column.reshape(groups, spans, 1) == own_links[None, None, :]
    expected = jnp.sum(jnp.where(found, member[None, :, None], 0), axis=1)
    expected = expected + spans * jnp.arange(groups, dtype=jnp.int32)[:, None]
    expected = jnp.pad(expected, ((0, 0), (0, 2 * block - rows_here)), constant_values=-1)

    marks = []
    planes = [col_ring(jnp.concatenate(line, axis=0), 1 - axis, marks) for axis, line in enumerate(lines)]
    chips, _ = lax.optimization_barrier(((own, on_1, on_2, on_3), marks))
    first_slab = swapped_slab(chips)
    panels = [(plane, axis) for axis, plane in enumerate(planes)]
    squares, table = first_product(
        None, expected, rows_at, groups_at, first_slab, panels, halves, spans, scale
    )
    second_slab = halves_slab(*squares, halves)
    all_strips = [[strip] for strip in halves]
    where = (table, rows_at, groups_at)
    return tuple(second_product(*where, second_slab, panels, all_strips, spans, scale, squares, own))


def solution(mesh):
    in_specs = (P("col", "row"), P(None, "col"))
    out_specs = (P("col", "row"), P("col", "row"))
    return jax.shard_map(
        per_device, mesh=mesh, in_specs=in_specs, out_specs=out_specs, check_vma=False
    )
```
